256 devices in a mesh: wide: 16 (over x, z_hi, core), narrow: 16 (over z_lo, y).
Axes of the slice: x: 4, y: 4, z: 8 (z_hi: 2, z_lo: 4; z = z_hi * 4 + z_lo), core: 2. Of those that a mesh axis runs over, the one named last changes fastest.
Arguments:
- inputs: bfloat16 [131072, 1024], P(('wide', 'narrow')), may hold values from -24 to 24
- w_first: bfloat16 [1024, 1024], replicated, may hold values from -0.1875 to 0.1875
- w_second: bfloat16 [1024, 256], replicated, may hold values from -0.1875 to 0.1875
- requests: int32 [4096, 128], P(('wide', 'narrow')), may hold values from 0 to 511
- slots: int32 [131072, 15], P(('wide', 'narrow')), may hold values from 0 to 2047
- counts: int32 [131072], P(('wide', 'narrow')), may hold values from 1 to 15
- edge_weight: int32 [131072, 15], P(('wide', 'narrow')), may hold values from 1 to 4
- offsets: int32 [4], replicated, may hold values from 0 to 511
Outputs:
- grad_first: float32 [1024, 1024], P('wide')
- grad_second: float32 [1024, 256], P('wide')
The draws below stay inside these ranges and needn't reach their ends.
Inputs may be any that keep to these rules, and one draw needn't show every extreme that they name: requests of block d only name rows of blocks with the same narrow index as d.
All inputs are finite; a program needn't handle non-finite values.
Results may differ from the reference program's by a relative error of at most 0.0018.
Values may be sent and summed in bfloat16 or wider, within the bound.
A program may use at most 64 MiB of HBM per device.

```python
import math
import jax
import jax.numpy as jnp
from jax import lax

ROWS = 512
DIN = 1024
HID = 1024
E = 256
K = 15
SHIFTS = 4
NEGW = 8
CAP = 128
ROWS_ALL = 131072
N_WIDE = 16
N_NARROW = 16


def plant(result, stream_key, low, largest):
    shape = result.shape
    spot = [jax.random.randint(jax.random.fold_in(stream_key, axis), (), 0, shape[axis]) for axis in range(len(shape))]
    result = result.at[tuple(spot)].set(low)
    longest = shape.index(max(shape))
    spot[longest] = (spot[longest] + 1) % shape[longest]
    return result.at[tuple(spot)].set(largest)


def raised(entries, stream_key, source, target, shards_of, factor):
    owner, partner = [(jnp.arange(entries.shape[position]) // (entries.shape[position] // shards_of)).reshape([-1 if axis == position else 1 for axis in range(entries.ndim)]) for position in (source, target)]
    chosen = jax.random.permutation(stream_key, shards_of)[partner]
    strong = (owner == chosen) | (owner == (partner + shards_of // 2) % shards_of)
    return jnp.where(strong, factor * entries, entries)


def block_scale(stream_key, extent, pieces, low, largest):
    level = 1.0
    for position, blocks in pieces:
        steps = jax.random.uniform(jax.random.fold_in(jax.random.fold_in(stream_key, 6), position), (blocks,), jnp.float32, low / len(pieces), largest / len(pieces))
        level = level * jnp.repeat(jnp.exp(steps), extent[position] // blocks).reshape((-1,) + (1,) * (len(extent) - 1 - position))
    return level


def noise(stream_key, extent, deviation, bound, shards=(), held_as=jnp.bfloat16):
    loudness = block_scale(stream_key, extent, shards, -0.22, 0.18) if shards else 1.0
    array = jax.random.normal(stream_key, extent, jnp.float32) * deviation * loudness
    return jnp.minimum(jnp.maximum(array, -bound), bound).astype(held_as)


def bell_draw_with(key, extent, width, most, shards, heavy, held_as=jnp.bfloat16):
    drawn = width * jax.random.normal(key, extent, jnp.float32)
    if shards:
        drawn = drawn * block_scale(key, extent, shards, -0.22, 0.18)
    return jnp.clip(raised(drawn, jax.random.fold_in(key, 3), *heavy), -most, most).astype(held_as)


def setup_inputs(seed: int = 0) -> dict:
    arg_keys = jax.random.split(jax.random.key(seed), 9)
    return {
        "inputs": bell_draw_with(arg_keys[0], (ROWS_ALL, DIN), 1.0, 24.0, ((0, 256),), (0, 1, 256, 6.0)),
        "w_first": noise(arg_keys[1], (DIN, HID), DIN ** -0.5, 0.1875),
        "w_second": noise(arg_keys[2], (HID, E), HID ** -0.5, 0.1875),
        "requests": plant(jax.random.randint(arg_keys[3], (N_WIDE * N_NARROW * N_WIDE, CAP), 0, ROWS), jax.random.fold_in(arg_keys[3], 1), 0, ROWS - 1).astype(jnp.int32),
        "slots": plant(jax.random.randint(arg_keys[4], (ROWS_ALL, K), 0, N_WIDE * CAP), jax.random.fold_in(arg_keys[4], 1), 0, (N_WIDE * CAP) - 1).astype(jnp.int32),
        "counts": plant(jax.random.randint(arg_keys[5], (ROWS_ALL,), 1, K + 1), jax.random.fold_in(arg_keys[5], 1), 1, K).astype(jnp.int32),
        "edge_weight": plant(jax.random.randint(arg_keys[6], (ROWS_ALL, K), 1, 5), jax.random.fold_in(arg_keys[6], 1), 1, 4).astype(jnp.int32),
        "offsets": plant(jax.random.randint(arg_keys[7], (SHIFTS,), 0, ROWS), jax.random.fold_in(arg_keys[7], 1), 0, ROWS - 1).astype(jnp.int32),
    }


def forward(block, w_first, w_second):
    pre = jnp.dot(block, w_first, preferred_element_type=jnp.float32)
    hidden = jnp.maximum(pre, 0.0).astype(jnp.bfloat16)
    codes = jnp.dot(hidden, w_second, preferred_element_type=jnp.float32)
    return (pre, hidden, codes)

def attract(codes, near, weight):
    diff = codes[:, None, :] - near.astype(jnp.float32)
    dist = lax.optimization_barrier(jnp.sum(diff * diff, axis=-1)) / diff.shape[-1]
    return lax.optimization_barrier(jnp.sum((weight / (1.0 + dist))[:, :, None] * diff, axis=1))

def repel(codes, far):
    diff = codes[:, None, :] - far.astype(jnp.float32)
    dist = lax.optimization_barrier(jnp.sum(diff * diff, axis=-1)) / diff.shape[-1]
    onep = 1.0 + dist
    coef = 1.0 / (onep * onep * (dist / onep + 0.1))
    return -lax.optimization_barrier(jnp.sum(coef[:, :, None] * diff, axis=1))

def negatives(block, offset, count):
    rows = block.shape[0]
    index = (jnp.arange(rows, dtype=jnp.int32)[:, None] + offset + jnp.arange(count, dtype=jnp.int32)[None, :]) % rows
    return block[index]

def reference(inputs, w_first, w_second, requests, slots, counts, edge_weight, offsets):
    devices = N_WIDE * N_NARROW
    blocks = inputs.reshape(devices, ROWS, DIN)

    def encode(block):
        return forward(block, w_first, w_second)[2].astype(jnp.bfloat16)
    sent = lax.map(encode, blocks)
    asked = requests.reshape(devices, N_WIDE, CAP)
    near_slots = slots.reshape(devices, ROWS, K)
    near_counts = counts.reshape(devices, ROWS)
    near_weight = edge_weight.reshape(devices, ROWS, K)
    scale = 2.0 / (K * math.sqrt(ROWS_ALL))

    def accumulate(carry, index):
        wide_idx = index // N_NARROW
        narrow_idx = index % N_NARROW
        pre, hidden, codes = forward(blocks[index], w_first, w_second)
        owners = jnp.arange(N_WIDE, dtype=jnp.int32) * N_NARROW + narrow_idx
        table = sent[owners[:, None], asked[index]].reshape(N_WIDE * CAP, E)
        near = table[near_slots[index]]
        live = jnp.arange(K, dtype=jnp.int32)[None, :] < near_counts[index][:, None]
        weight = jnp.where(live, near_weight[index].astype(jnp.float32), jnp.float32(0.0))
        grad = attract(codes, near, weight)
        for step in range(SHIFTS):
            source = wide_idx * N_NARROW + (narrow_idx - step - 1) % N_NARROW
            grad = grad + repel(codes, negatives(sent[source], offsets[step], NEGW))
        dcodes = (scale * grad).astype(jnp.bfloat16)
        part_second = jnp.dot(hidden.T, dcodes, preferred_element_type=jnp.float32)
        dhidden = jnp.dot(dcodes, w_second.T, preferred_element_type=jnp.float32)
        dpre = jnp.where(pre > 0, dhidden, jnp.float32(0.0)).astype(jnp.bfloat16)
        part_first = jnp.dot(blocks[index].T, dpre, preferred_element_type=jnp.float32)
        return ((carry[0] + part_first, carry[1] + part_second), None)
    start = (jnp.zeros((DIN, HID), jnp.float32), jnp.zeros((HID, E), jnp.float32))
    (grad_first, grad_second), _ = lax.scan(accumulate, start, jnp.arange(devices, dtype=jnp.int32))
    return (grad_first, grad_second)
```

```python
import math

import jax
import jax.numpy as jnp
from jax import lax
from jax.experimental import pallas as pl
from jax.experimental.pallas import tpu as pltpu
from jax.sharding import PartitionSpec as P

MESH = pl.DeviceIdType.MESH
F32 = jnp.float32
BF16 = jnp.bfloat16
NEGW = 8
NX, NH, NC, NL, NY = 4, 2, 2, 4, 4


def nt(a, b):
    return lax.dot_general(a, b, (((1,), (1,)), ((), ())), preferred_element_type=F32)


def nn(a, b):
    return jnp.dot(a, b, preferred_element_type=F32)


def step(
    scale, inputs, w1, w2, requests, slots, counts, edges, offsets, out_first, out_second,
    hidden, codes, sent, mate, far, reqs, asked, keys, found, table, weights, norms,
    xt, ht, sums, acc, dist, coef, dpre, dcodes, ga, gb,
    ca_out, ca_in, cb_out, cb_in, pa1_out, pa1_in, pb1_out, pb1_in, fa1, fb1,
    pa2_out, pa2_in, pb2_out, pb2_in, zs_out, zs_in, whole, send_sem, recv_sem,
):
    w = lax.axis_index("wide")
    n = lax.axis_index("narrow")
    x, h, c = w // 4, (w // 2) % 2, w % 2
    l, y = n // 4, n % 4
    rows = inputs.shape[0]
    sem_count = [0]

    def device(xx, hh, cc, ll, yy):
        return (xx * 4 + hh * 2 + cc, ll * 4 + yy)

    def copy(src, dst, target):
        at = sem_count[0]
        sem_count[0] += 1
        return pltpu.make_async_remote_copy(
            src_ref=src, dst_ref=dst, send_sem=send_sem.at[at], recv_sem=recv_sem.at[at],
            device_id=target, device_id_type=MESH,
        )

    def xs(s):
        return (x + s) % NX

    def ys(s):
        return (y + s) % NY

    def ls(s):
        return (l + s) % NL

    barrier = pltpu.get_barrier_semaphore()
    plane = [(dx, dc) for dx in range(NX) for dc in range(NC) if dx or dc]
    ring = [(dl, dy) for dl in range(NL) for dy in range(NY) if dl or dy]
    peers = [device(xs(dx), h, (c + dc) % 2, l, y) for dx, dc in plane]
    peers += [device(x, h, c, ls(dl), ys(dy)) for dl, dy in ring]
    peers += [device(x, 1 - h, c, ls(dl), y) for dl in range(NL)]
    for peer in peers:
        pl.semaphore_signal(barrier, inc=1, device_id=peer, device_id_type=MESH)

    reqs[...] = jnp.zeros_like(reqs)
    for xx in range(NX):
        for cc in range(NC):
            for hh in range(NH):
                p = xx * 4 + hh * 2 + cc
                reqs[xx * 2 + cc, hh : hh + 1, :] = requests[p : p + 1, :]

    for at in range(0, 1024, 256):
        pre = nn(inputs[...], w1[:, at : at + 256])
        hidden[:, at : at + 256] = jnp.maximum(pre, 0.0).astype(BF16)
    codes[...] = nn(hidden[...], w2[...])
    sent[...] = codes[...].astype(BF16)

    pl.semaphore_wait(barrier, len(peers))

    ask = []
    for dx, dc in plane:
        j = dx * 2 + dc
        cp = copy(reqs.at[xs(dx) * 2 + (c + dc) % 2], asked.at[j], device(xs(dx), h, (c + dc) % 2, l, y))
        cp.start()
        ask.append(cp)
    to_next = copy(sent, far.at[3], device(x, h, c, ls(1), y))
    to_next.start()
    to_mate = copy(sent, mate, device(x, 1 - h, c, l, y))
    to_mate.start()
    to_y = []
    for s in (1, 2, 3):
        cp = copy(sent, far.at[s - 1], device(x, h, c, l, ys(s)))
        to_y.append(cp)
        pl.when(y + s < NY)(cp.start)

    live = lax.broadcasted_iota(jnp.int32, slots.shape, 0) < counts[...]
    keys[...] = jnp.zeros_like(keys)
    keys[0:15, :] = slots[...].astype(F32)
    keys[16:31, :] = jnp.where(live, edges[...], 0).astype(F32)
    norms[...] = keys[...].T

    def weigh(at, _):
        r = pl.multiple_of(at * 16, 16)
        both = norms[pl.ds(r, 16), :]
        lane = lax.broadcasted_iota(jnp.int32, (16, 512), 1).astype(F32)
        spots = [jnp.broadcast_to(both[:, k : k + 1], (16, 512)) for k in range(15)]
        worth = [jnp.broadcast_to(both[:, 16 + k : 17 + k], (16, 512)) for k in range(15)]
        for part in range(4):
            total = jnp.zeros((16, 512), F32)
            for k in range(15):
                total = total + jnp.where(spots[k] == lane + float(part * 512), worth[k], 0.0)
            weights[part, pl.ds(r, 16), :] = total.astype(BF16)
        return 0

    lax.fori_loop(0, rows // 32, weigh, 0)

    for cp in ask:
        cp.wait_recv()
    asked[0] = reqs[x * 2 + c]
    for j in range(8):
        norms2 = asked[j]
        keys[j * 8 : j * 8 + 8, 0:128] = norms2.astype(F32)
    wanted = keys[:, 0:128].T

    reply = []

    def serve(block, b):
        lane = lax.broadcasted_iota(jnp.int32, (128, rows), 1).astype(F32)
        for j in (2, 6, 4, 3, 7, 5, 1, 0):
            dx, dc = j // 2, j % 2
            col = j * 8
            which = jnp.where(b == 0, wanted[:, col : col + 1], wanted[:, col + 1 : col + 2])
            pick = jnp.where(jnp.broadcast_to(which, (128, rows)) == lane, 1.0, 0.0).astype(BF16)
            got = nn(pick, block[...]).astype(BF16)
            if j == 0:
                table[x, pl.ds(pl.multiple_of(b * 256 + c * 128, 128), 128), :] = got
            else:
                slot = (j - 1) * 2
                found[slot + (0 if block is sent else 1)] = got
                cp = copy(
                    found.at[slot + (0 if block is sent else 1)],
                    table.at[x, pl.ds(pl.multiple_of(b * 256 + c * 128, 128), 128), :],
                    device(xs(NX - dx), h, (c + dc) % 2, l, y),
                )
                cp.start()
                reply.append((dx, cp))

    serve(sent, h)
    to_next.wait_recv()
    for s in (1, 2, 3):
        cp = pltpu.make_async_remote_copy(
            src_ref=far.at[3], dst_ref=far.at[s - 1], send_sem=send_sem.at[9 + s - 1],
            recv_sem=recv_sem.at[9 + s - 1], device_id=device(x, h, c, l, ys(s)), device_id_type=MESH,
        )
        pl.when(y + s >= NY)(cp.start)
    lax.fori_loop(rows // 32, rows // 16, weigh, 0)
    for g in range(8):
        xt[g * 128 : g * 128 + 128, :] = inputs[:, g * 128 : g * 128 + 128].T
        ht[g * 128 : g * 128 + 128, :] = hidden[:, g * 128 : g * 128 + 128].T
    to_mate.wait_recv()
    serve(mate, 1 - h)

    own = sent[...].astype(F32)
    norm = jnp.sum(own * own, axis=1, keepdims=True)
    norms[...] = jnp.broadcast_to(norm, norms.shape)
    sums[...] = jnp.zeros_like(sums)
    acc[...] = jnp.zeros_like(acc)
    ones = jnp.ones((8, 256), BF16)
    inv = 1.0 / 256.0

    def squares(block):
        z = block.astype(F32)
        z = z * z
        hi = z.astype(BF16)
        lo = (z - hi.astype(F32)).astype(BF16)
        return (nt(ones, hi) + nt(ones, lo))[0:1, :]

    def pull(block, part, kind, offset):
        dist[...] = nt(sent[...], block)
        size = squares(block)

        def tile(at, _):
            r = pl.multiple_of(at * 32, 32)
            mine = norms[pl.ds(r, 32), :]
            total = sums[pl.ds(r, 32), :]
            for q in range(4):
                cols = slice(q * 128, q * 128 + 128)
                d = jnp.maximum((mine + size[:, cols]) - 2.0 * dist[pl.ds(r, 32), cols], 0.0) * inv
                if kind == "near":
                    k = weights[part, pl.ds(r, 32), cols].astype(F32) / (1.0 + d)
                else:
                    i = lax.broadcasted_iota(jnp.int32, (32, 128), 0)
                    j = lax.broadcasted_iota(jnp.int32, (32, 128), 1)
                    band = ((j - i) + (q * 128 - r - offset)) & (rows - 1)
                    k = jnp.where(band < NEGW, -1.0 / ((1.0 + d) * (1.1 * d + 0.1)), 0.0)
                k = k.astype(BF16)
                coef[pl.ds(r, 32), cols] = k
                total = total + k.astype(F32)
            sums[pl.ds(r, 32), :] = total
            return 0

        lax.fori_loop(0, rows // 32, tile, 0)
        acc[...] += nn(coef[...], block)

    pull(far[3], None, "far", offsets[3])
    for s in (1, 3, 2):
        to_y[s - 1].wait_recv()
        pull(far[s - 1], None, "far", offsets[s - 1])
    for dx in (0, 1, 3, 2):
        for at, cp in reply:
            if at == dx:
                cp.wait_recv()
        part = xs(dx)
        pull(table[part], part, "near", None)

    total = jnp.sum(sums[...], axis=1, keepdims=True)
    dcodes[...] = (scale * (total * codes[...] - acc[...])).astype(BF16)

    core = device(x, h, 1 - c, l, y)
    second = nn(ht[...], dcodes[...])
    ga[:, 512:640] = second[:, 0:128]
    gb[:, 512:640] = second[:, 128:256]

    def backward(g, first):
        for at in range(first, first + 512, 256):
            back = nt(dcodes[...], w2[at : at + 256, :])
            dpre[:, at : at + 256] = jnp.where(hidden[:, at : at + 256] > 0, back, 0.0).astype(BF16)
            g[:, at - first : at - first + 256] = nn(xt[...], dpre[:, at : at + 256])

    def part_rows(xx, hh, cc, yy):
        return pl.ds(pl.multiple_of(xx * 256 + hh * 128 + cc * 64 + yy * 16, 16), 16)

    backward(gb, 512)
    for xx in range(NX):
        for hh in range(NH):
            for yy in range(NY):
                cb_out[yy, xx, hh] = gb[part_rows(xx, hh, 1 - c, yy), :].astype(BF16)
    core_b = copy(cb_out, cb_in, core)
    core_b.start()
    backward(ga, 0)
    for xx in range(NX):
        for hh in range(NH):
            for yy in range(NY):
                ca_out[xx, hh, yy] = ga[part_rows(xx, hh, 1 - c, yy), :].astype(BF16)
    core_a = copy(ca_out, ca_in, core)
    core_a.start()

    core_b.wait_recv()
    for yy in range(NY):
        for xx in range(NX):
            for hh in range(NH):
                both = gb[part_rows(xx, hh, c, yy), :] + cb_in[yy, xx, hh].astype(F32)
                pb1_out[yy, xx, hh] = both.astype(BF16)
    b1 = []
    for s in (1, 2, 3):
        cp = copy(pb1_out.at[ys(s)], pb1_in.at[s - 1], device(x, h, c, l, ys(s)))
        cp.start()
        b1.append(cp)
    core_a.wait_recv()
    for xx in range(NX):
        for hh in range(NH):
            for yy in range(NY):
                both = ga[part_rows(xx, hh, c, yy), :] + ca_in[xx, hh, yy].astype(F32)
                pa1_out[xx, hh, yy] = both.astype(BF16)
    a1 = []
    for s in (1, 2, 3):
        cp = copy(pa1_out.at[xs(s)], pa1_in.at[s - 1], device(xs(s), h, c, l, y))
        cp.start()
        a1.append(cp)
    for xx in range(NX):
        for hh in range(NH):
            fb1[xx, hh] = gb[part_rows(xx, hh, c, y), :] + cb_in[y, xx, hh].astype(F32)
    for hh in range(NH):
        for yy in range(NY):
            fa1[yy, hh] = ga[part_rows(x, hh, c, yy), :] + ca_in[x, hh, yy].astype(F32)

    for cp in b1:
        cp.wait_recv()
    for xx in range(NX):
        for hh in range(NH):
            got = [pb1_in[s, xx, hh].astype(F32) for s in range(3)]
            fb1[xx, hh] += got[0] + got[1] + got[2]
            pb2_out[xx, hh] = fb1[xx, hh].astype(BF16)
    b2 = []
    for s in (1, 2, 3):
        cp = copy(pb2_out.at[xs(s)], pb2_in.at[s - 1], device(xs(s), h, c, l, y))
        cp.start()
        b2.append(cp)
    for cp in a1:
        cp.wait_recv()
    for yy in range(NY):
        for hh in range(NH):
            got = [pa1_in[s, hh, yy].astype(F32) for s in range(3)]
            fa1[yy, hh] += got[0] + got[1] + got[2]
            pa2_out[yy, hh] = fa1[yy, hh].astype(BF16)
    a2 = []
    for s in (1, 2, 3):
        cp = copy(pa2_out.at[ys(s)], pa2_in.at[s - 1], device(x, h, c, l, ys(s)))
        cp.start()
        a2.append(cp)
    for cp in b2 + a2:
        cp.wait_recv()
    for hh in range(NH):
        for half, mine, got in ((0, fa1[y, hh], pa2_in), (1, fb1[x, hh], pb2_in)):
            total = mine + got[0, hh].astype(F32) + got[1, hh].astype(F32) + got[2, hh].astype(F32)
            zs_out[hh, half] = total[0:8, :]
            zs_out[hh, 2 + half] = total[8:16, :]

    zs = []
    for dh in range(NH):
        for dl in range(NL):
            if dh or dl:
                hh = (h + dh) % 2
                cp = copy(zs_out.at[hh, ls(dl)], zs_in.at[dh * 4 + dl], device(x, hh, c, ls(dl), y))
                cp.start()
                zs.append(cp)
    total = zs_out[h, l]
    for cp in zs:
        cp.wait_recv()
    for j in range(1, 8):
        total = total + zs_in[j]
    whole[y, l] = total
    spread = []
    for dl, dy in ring:
        cp = copy(whole.at[y, l], whole.at[y, l], device(x, h, c, ls(dl), ys(dy)))
        cp.start()
        spread.append(cp)
    for cp in spread:
        cp.wait_recv()
    for yy in range(NY):
        for ll in range(NL):
            r = yy * 16 + (ll // 2) * 8
            half = ll % 2
            out_first[r : r + 8, half * 512 : half * 512 + 512] = whole[yy, ll, :, 0:512]
            out_second[r : r + 8, half * 128 : half * 128 + 128] = whole[yy, ll, :, 512:640]

    for cp in ask + [to_next, to_mate] + to_y + [cp for _, cp in reply] + [core_a, core_b]:
        cp.wait_send()
    for cp in a1 + b1 + a2 + b2 + zs + spread:
        cp.wait_send()


def shards(inputs, w_first, w_second, requests, slots, counts, edge_weight, offsets):
    rows = inputs.shape[0]
    total_rows = rows * lax.axis_size("wide") * lax.axis_size("narrow")
    scale = 2.0 / (slots.shape[1] * math.sqrt(total_rows))
    vmem = pl.BlockSpec(memory_space=pltpu.VMEM)
    smem = pl.BlockSpec(memory_space=pltpu.SMEM)
    return pl.pallas_call(
        lambda *refs: step(scale, *refs),
        out_shape=(jax.ShapeDtypeStruct((64, 1024), F32), jax.ShapeDtypeStruct((64, 256), F32)),
        in_specs=[vmem] * 7 + [smem],
        out_specs=(vmem, vmem),
        scratch_shapes=[
            pltpu.VMEM((512, 1024), BF16),
            pltpu.VMEM((512, 256), F32),
            pltpu.VMEM((512, 256), BF16),
            pltpu.VMEM((512, 256), BF16),
            pltpu.VMEM((4, 512, 256), BF16),
            pltpu.VMEM((8, 8, 128), jnp.int32),
            pltpu.VMEM((8, 8, 128), jnp.int32),
            pltpu.VMEM((128, 512), F32),
            pltpu.VMEM((14, 128, 256), BF16),
            pltpu.VMEM((4, 512, 256), BF16),
            pltpu.VMEM((4, 512, 512), BF16),
            pltpu.VMEM((512, 128), F32),
            pltpu.VMEM((1024, 512), BF16),
            pltpu.VMEM((1024, 512), BF16),
            pltpu.VMEM((512, 128), F32),
            pltpu.VMEM((512, 256), F32),
            pltpu.VMEM((512, 512), F32),
            pltpu.VMEM((512, 512), BF16),
            pltpu.VMEM((512, 1024), BF16),
            pltpu.VMEM((512, 256), BF16),
            pltpu.VMEM((1024, 640), F32),
            pltpu.VMEM((1024, 640), F32),
            pltpu.VMEM((4, 2, 4, 16, 640), BF16),
            pltpu.VMEM((4, 2, 4, 16, 640), BF16),
            pltpu.VMEM((4, 4, 2, 16, 640), BF16),
            pltpu.VMEM((4, 4, 2, 16, 640), BF16),
            pltpu.VMEM((4, 2, 4, 16, 640), BF16),
            pltpu.VMEM((3, 2, 4, 16, 640), BF16),
            pltpu.VMEM((4, 4, 2, 16, 640), BF16),
            pltpu.VMEM((3, 4, 2, 16, 640), BF16),
            pltpu.VMEM((4, 2, 16, 640), F32),
            pltpu.VMEM((4, 2, 16, 640), F32),
            pltpu.VMEM((4, 2, 16, 640), BF16),
            pltpu.VMEM((3, 2, 16, 640), BF16),
            pltpu.VMEM((4, 2, 16, 640), BF16),
            pltpu.VMEM((3, 2, 16, 640), BF16),
            pltpu.VMEM((2, 4, 8, 640), F32),
            pltpu.VMEM((8, 8, 640), F32),
            pltpu.VMEM((4, 4, 8, 640), F32),
            pltpu.SemaphoreType.DMA((64,)),
            pltpu.SemaphoreType.DMA((64,)),
        ],
        compiler_params=pltpu.CompilerParams(
            collective_id=0, has_side_effects=True, vmem_limit_bytes=56 << 20
        ),
        cost_estimate=pl.CostEstimate(flops=9_000_000_000, bytes_accessed=5_000_000, transcendentals=0),
        name="embedding_step",
    )(
        inputs, w_first, w_second, requests, slots.T, counts.reshape(1, -1), edge_weight.T, offsets
    )


def solution(mesh):
    return jax.shard_map(
        shards,
        mesh=mesh,
        in_specs=(
            P(("wide", "narrow"), None),
            P(),
            P(),
            P(("wide", "narrow"), None),
            P(("wide", "narrow"), None),
            P(("wide", "narrow")),
            P(("wide", "narrow"), None),
            P(),
        ),
        out_specs=(P("wide", None), P("wide", None)),
        check_vma=False,
    )
```

```python
import math

import jax
import jax.numpy as jnp
from jax import lax
from jax.experimental import pallas as pl
from jax.experimental.pallas import tpu as pltpu
from jax.sharding import PartitionSpec as P

MESH = pl.DeviceIdType.MESH
F32 = jnp.float32
BF16 = jnp.bfloat16
NEGW = 8
NX, NH, NC, NL, NY = 4, 2, 2, 4, 4


def nt(a, b):
    return lax.dot_general(a, b, (((1,), (1,)), ((), ())), preferred_element_type=F32)


def nn(a, b):
    return jnp.dot(a, b, preferred_element_type=F32)


def step(
    scale, inputs_hbm, w1_hbm, w2_hbm, requests_hbm, slots_hbm, counts_hbm, edges_hbm, offsets, out,
    inputs, w1, w2, requests, slots, counts, edges, in_sem, picks, sent_part, hidden, codes, sent, mate, far, reqs, asked, keys, found, table, weights, norms,
    xt, ht, sums, acc, dist, coef, dpre, dcodes, ga, gb,
    ca_out, ca_in, cb_out, cb_in, pa1_out, pa1_in, pb1_out, pb1_in, fa1, fb1,
    pa2_out, pa2_in, pb2_out, pb2_in, zs_out, zs_in, whole, send_sem, recv_sem,
):
    w = lax.axis_index("wide")
    n = lax.axis_index("narrow")
    x, h, c = w // 4, (w // 2) % 2, w % 2
    l, y = n // 4, n % 4
    rows = inputs.shape[0]
    sem_count = [0]

    loads = []
    for at, (src, dst) in enumerate((
        (inputs_hbm, inputs), (requests_hbm, requests),
        (w1_hbm.at[:, 0:256], w1.at[:, 0:256]), (w1_hbm.at[:, 256:512], w1.at[:, 256:512]),
        (w1_hbm.at[:, 512:768], w1.at[:, 512:768]), (w1_hbm.at[:, 768:1024], w1.at[:, 768:1024]),
        (w2_hbm, w2), (slots_hbm, slots), (counts_hbm, counts), (edges_hbm, edges),
    )):
        load = pltpu.make_async_copy(src, dst, in_sem.at[at])
        load.start()
        loads.append(load)

    def device(xx, hh, cc, ll, yy):
        return (xx * 4 + hh * 2 + cc, ll * 4 + yy)

    def copy(src, dst, target):
        at = sem_count[0]
        sem_count[0] += 1
        return pltpu.make_async_remote_copy(
            src_ref=src, dst_ref=dst, send_sem=send_sem.at[at], recv_sem=recv_sem.at[at],
            device_id=target, device_id_type=MESH,
        )

    def xs(s):
        return (x + s) % NX

    def ys(s):
        return (y + s) % NY

    def ls(s):
        return (l + s) % NL

    barrier = pltpu.get_barrier_semaphore()
    plane = [(dx, dc) for dx in range(NX) for dc in range(NC) if dx or dc]
    ring = [(dl, dy) for dl in range(NL) for dy in range(NY) if dl or dy]
    peers = [device(xs(dx), h, (c + dc) % 2, l, y) for dx, dc in plane]
    peers += [device(x, h, c, ls(dl), ys(dy)) for dl, dy in ring]
    peers += [device(x, 1 - h, c, ls(dl), y) for dl in range(NL)]
    for peer in peers:
        pl.semaphore_signal(barrier, inc=1, device_id=peer, device_id_type=MESH)

    loads[1].wait()
    reqs[...] = jnp.zeros_like(reqs)
    for xx in range(NX):
        for cc in range(NC):
            for hh in range(NH):
                p = xx * 4 + hh * 2 + cc
                reqs[xx * 2 + cc, hh : hh + 1, :] = requests[p : p + 1, :]

    loads[0].wait()
    for at in range(0, 1024, 256):
        loads[2 + at // 256].wait()
        pre = nn(inputs[...], w1[:, at : at + 256])
        hidden[:, at : at + 256] = jnp.maximum(pre, 0.0).astype(BF16)
    loads[6].wait()
    codes[...] = nn(hidden[...], w2[...])
    sent[...] = codes[...].astype(BF16)
    sent_part[...] = sent[...] * (2.0 / 256.0)

    pl.semaphore_wait(barrier, len(peers))

    ask = []
    for dx, dc in plane:
        j = dx * 2 + dc
        cp = copy(reqs.at[xs(dx) * 2 + (c + dc) % 2], asked.at[j], device(xs(dx), h, (c + dc) % 2, l, y))
        cp.start()
        ask.append(cp)
    to_next = copy(sent, far.at[3], device(x, h, c, ls(1), y))
    to_next.start()
    to_mate = []
    for e in range(2):
        cols = slice(e * 128, e * 128 + 128)
        cp = copy(sent.at[:, cols], mate.at[:, cols], device(x, 1 - h, c, l, y))
        cp.start()
        to_mate.append(cp)
    to_y = []
    for s in (1, 2, 3):
        cp = copy(sent, far.at[s - 1], device(x, h, c, l, ys(s)))
        to_y.append(cp)
        pl.when(y + s < NY)(cp.start)

    for load in loads[7:]:
        load.wait()
    live = lax.broadcasted_iota(jnp.int32, slots.shape, 0) < counts[...]
    keys[...] = jnp.zeros_like(keys)
    place = ((slots[...] - x * 512) & 2047) ^ (h * 256 + c * 128)
    keys[0:15, :] = place.astype(F32)
    keys[16:31, :] = jnp.where(live, edges[...], 0).astype(F32)
    norms[...] = keys[...].T

    def weigh(at, _):
        r = pl.multiple_of(at * 16, 16)
        both = norms[pl.ds(r, 16), :]
        lane = lax.broadcasted_iota(jnp.int32, (16, 512), 1).astype(F32)
        spots = [jnp.broadcast_to(both[:, k : k + 1], (16, 512)) for k in range(15)]
        worth = [jnp.broadcast_to(both[:, 16 + k : 17 + k], (16, 512)) for k in range(15)]
        for part in range(4):
            total = jnp.zeros((16, 512), F32)
            for k in range(15):
                total = total + jnp.where(spots[k] == lane + float(part * 512), worth[k], 0.0)
            weights[part, pl.ds(r, 16), :] = total.astype(BF16)
        return 0

    lax.fori_loop(0, rows // 32, weigh, 0)

    for cp in ask:
        cp.wait_recv()
    asked[0] = reqs[x * 2 + c]
    for j in range(8):
        norms2 = asked[j]
        keys[j * 8 : j * 8 + 8, 0:128] = norms2.astype(F32)
    wanted = keys[:, 0:128].T

    lane = lax.broadcasted_iota(jnp.int32, (128, rows), 1).astype(F32)
    reply = {}

    def deliver(block, b, j, e):
        cols = slice(0, 256) if e is None else slice(e * 128, e * 128 + 128)
        got = nn(picks[b, j], block[:, cols]).astype(BF16)
        dx, dc = j // 2, j % 2
        spot = slice(b * 256 + dc * 128, b * 256 + dc * 128 + 128)
        if j == 0:
            table[0, spot, cols] = got
        else:
            found[b, j - 1, :, cols] = got
            cp = copy(
                found.at[b, j - 1, :, cols], table.at[dx, spot, cols],
                device(xs(NX - dx), h, (c + dc) % 2, l, y),
            )
            cp.start()
            reply.setdefault((b, dx), []).append(cp)

    turns = (2, 6, 4, 3, 7, 5, 1, 0)
    for b in range(2):
        for j in turns:
            which = jnp.where((h + b) % 2 == 0, wanted[:, j * 8 : j * 8 + 1], wanted[:, j * 8 + 1 : j * 8 + 2])
            picks[b, j] = jnp.where(jnp.broadcast_to(which, (128, rows)) == lane, 1.0, 0.0).astype(BF16)
            if b == 0:
                deliver(sent, 0, j, None)
    to_next.wait_recv()
    for s in (1, 2, 3):
        cp = pltpu.make_async_remote_copy(
            src_ref=far.at[3], dst_ref=far.at[s - 1], send_sem=send_sem.at[10 + s - 1],
            recv_sem=recv_sem.at[10 + s - 1], device_id=device(x, h, c, l, ys(s)), device_id_type=MESH,
        )
        pl.when(y + s >= NY)(cp.start)
    lax.fori_loop(rows // 32, rows // 16, weigh, 0)
    for g in range(8):
        xt[g * 128 : g * 128 + 128, :] = inputs[:, g * 128 : g * 128 + 128].T
        ht[g * 128 : g * 128 + 128, :] = hidden[:, g * 128 : g * 128 + 128].T

    inv = 1.0 / 256.0
    own = sent[...].astype(F32)
    norm = jnp.sum(own * own, axis=1, keepdims=True)
    norms[...] = jnp.broadcast_to(norm * inv + 1.0, norms.shape)
    sums[...] = jnp.zeros_like(sums)
    acc[...] = jnp.zeros_like(acc)
    ones = jnp.ones((8, 256), BF16)

    def squares(block):
        z = block.astype(F32)
        z = z * z
        hi = z.astype(BF16)
        lo = (z - hi.astype(F32)).astype(BF16)
        return (nt(ones, hi) + nt(ones, lo))[0:1, :] * inv

    def pull(block, dx, b, offset):
        wide = block.shape[0]
        dist[:, 0:wide] = nt(sent_part[...], block[...])
        size = squares(block[...])

        def tile(at, _):
            r = pl.multiple_of(at * 64, 64)
            mine = norms[pl.ds(r, 64), :]
            total = sums[pl.ds(r, 64), :]
            for q in range(wide // 128):
                cols = slice(q * 128, q * 128 + 128)
                d = jnp.maximum((mine + size[:, cols]) - dist[pl.ds(r, 64), cols], 1.0)
                if dx is not None:
                    at_b = slice(b * 256 + q * 128, b * 256 + q * 128 + 128)
                    k = weights[dx, pl.ds(r, 64), at_b].astype(F32) * (1.0 / d)
                else:
                    i = lax.broadcasted_iota(jnp.int32, (64, 128), 0)
                    j = lax.broadcasted_iota(jnp.int32, (64, 128), 1)
                    band = ((j - i) + (q * 128 - r - offset)) & (rows - 1)
                    k = jnp.where(band < NEGW, -1.0 / (d * (1.1 * (d - 1.0) + 0.1)), 0.0)
                k = k.astype(BF16)
                coef[pl.ds(r, 64), cols] = k
                total = total + k.astype(F32)
            sums[pl.ds(r, 64), :] = total
            return 0

        lax.fori_loop(0, rows // 64, tile, 0)
        acc[...] += nn(coef[:, 0:wide], block[...])

    def attract(b):
        for dx in (0, 1, 3, 2):
            for cp in reply[b, dx]:
                cp.wait_recv()
            pull(table.at[dx, b * 256 : b * 256 + 256], dx, b, None)

    attract(0)
    for e in range(2):
        to_mate[e].wait_recv()
        for j in turns:
            deliver(mate, 1, j, e)
    pull(far.at[3], None, None, offsets[3])
    for s in (1, 3, 2):
        to_y[s - 1].wait_recv()
        pull(far.at[s - 1], None, None, offsets[s - 1])
    attract(1)

    total = jnp.sum(sums[...], axis=1, keepdims=True)
    dcodes[...] = (scale * (total * codes[...] - acc[...])).astype(BF16)

    core = device(x, h, 1 - c, l, y)
    second = nn(ht[...], dcodes[...])
    ga[:, 512:640] = second[:, 0:128]
    gb[:, 512:640] = second[:, 128:256]

    def backward(g, first):
        for at in range(first, first + 512, 256):
            back = nt(dcodes[...], w2[at : at + 256, :])
            dpre[:, at : at + 256] = jnp.where(hidden[:, at : at + 256] > 0, back, 0.0).astype(BF16)
            g[:, at - first : at - first + 256] = nn(xt[...], dpre[:, at : at + 256])

    def part_rows(xx, hh, cc, yy):
        return pl.ds(pl.multiple_of(xx * 256 + hh * 128 + cc * 64 + yy * 16, 16), 16)

    backward(gb, 512)
    for xx in range(NX):
        for hh in range(NH):
            for yy in range(NY):
                cb_out[yy, xx, hh] = gb[part_rows(xx, hh, 1 - c, yy), :].astype(BF16)
    core_b = copy(cb_out, cb_in, core)
    core_b.start()
    backward(ga, 0)
    for xx in range(NX):
        for hh in range(NH):
            for yy in range(NY):
                ca_out[xx, hh, yy] = ga[part_rows(xx, hh, 1 - c, yy), :].astype(BF16)
    core_a = copy(ca_out, ca_in, core)
    core_a.start()

    core_b.wait_recv()
    for yy in range(NY):
        for xx in range(NX):
            for hh in range(NH):
                both = gb[part_rows(xx, hh, c, yy), :] + cb_in[yy, xx, hh].astype(F32)
                pb1_out[yy, xx, hh] = both.astype(BF16)
    b1 = []
    for s in (1, 2, 3):
        cp = copy(pb1_out.at[ys(s)], pb1_in.at[s - 1], device(x, h, c, l, ys(s)))
        cp.start()
        b1.append(cp)
    core_a.wait_recv()
    for xx in range(NX):
        for hh in range(NH):
            for yy in range(NY):
                both = ga[part_rows(xx, hh, c, yy), :] + ca_in[xx, hh, yy].astype(F32)
                pa1_out[xx, hh, yy] = both.astype(BF16)
    a1 = []
    for s in (1, 2, 3):
        cp = copy(pa1_out.at[xs(s)], pa1_in.at[s - 1], device(xs(s), h, c, l, y))
        cp.start()
        a1.append(cp)
    for xx in range(NX):
        for hh in range(NH):
            fb1[xx, hh] = gb[part_rows(xx, hh, c, y), :] + cb_in[y, xx, hh].astype(F32)
    for hh in range(NH):
        for yy in range(NY):
            fa1[yy, hh] = ga[part_rows(x, hh, c, yy), :] + ca_in[x, hh, yy].astype(F32)

    for cp in b1:
        cp.wait_recv()
    for xx in range(NX):
        for hh in range(NH):
            got = [pb1_in[s, xx, hh].astype(F32) for s in range(3)]
            fb1[xx, hh] += got[0] + got[1] + got[2]
            pb2_out[xx, hh] = fb1[xx, hh].astype(BF16)
    b2 = []
    for s in (1, 2, 3):
        cp = copy(pb2_out.at[xs(s)], pb2_in.at[s - 1], device(xs(s), h, c, l, y))
        cp.start()
        b2.append(cp)
    for cp in a1:
        cp.wait_recv()
    for yy in range(NY):
        for hh in range(NH):
            got = [pa1_in[s, hh, yy].astype(F32) for s in range(3)]
            fa1[yy, hh] += got[0] + got[1] + got[2]
            pa2_out[yy, hh] = fa1[yy, hh].astype(BF16)
    a2 = []
    for s in (1, 2, 3):
        cp = copy(pa2_out.at[ys(s)], pa2_in.at[s - 1], device(x, h, c, l, ys(s)))
        cp.start()
        a2.append(cp)
    for cp in b2 + a2:
        cp.wait_recv()
    for hh in range(NH):
        for half, mine, got in ((0, fa1[y, hh], pa2_in), (1, fb1[x, hh], pb2_in)):
            total = mine + got[0, hh].astype(F32) + got[1, hh].astype(F32) + got[2, hh].astype(F32)
            zs_out[hh, half] = total[0:8, :]
            zs_out[hh, 2 + half] = total[8:16, :]

    zs = []
    for dh in range(NH):
        for dl in range(NL):
            if dh or dl:
                hh = (h + dh) % 2
                cp = copy(zs_out.at[hh, ls(dl)], zs_in.at[dh * 4 + dl], device(x, hh, c, ls(dl), y))
                cp.start()
                zs.append(cp)
    total = zs_out[h, l]
    for cp in zs:
        cp.wait_recv()
    for j in range(1, 8):
        total = total + zs_in[j]
    whole[y, l] = total
    spread = []
    for dl, dy in ring:
        cp = copy(whole.at[y, l], whole.at[y, l], device(x, h, c, ls(dl), ys(dy)))
        cp.start()
        spread.append(cp)
    for cp in spread:
        cp.wait_recv()
    out[...] = whole[...]

    for cp in ask + [to_next] + to_mate + to_y + sum(reply.values(), []) + [core_a, core_b]:
        cp.wait_send()
    for cp in a1 + b1 + a2 + b2 + zs + spread:
        cp.wait_send()


def assemble(whole, out_first, out_second):
    for yy in range(NY):
        for ll in range(NL):
            r = yy * 16 + (ll // 2) * 8
            half = ll % 2
            out_first[r : r + 8, half * 512 : half * 512 + 512] = whole[yy, ll, :, 0:512]
            out_second[r : r + 8, half * 128 : half * 128 + 128] = whole[yy, ll, :, 512:640]


def shards(inputs, w_first, w_second, requests, slots, counts, edge_weight, offsets):
    rows = inputs.shape[0]
    total_rows = rows * lax.axis_size("wide") * lax.axis_size("narrow")
    scale = 2.0 / (slots.shape[1] * math.sqrt(total_rows))
    vmem = pl.BlockSpec(memory_space=pltpu.VMEM)
    smem = pl.BlockSpec(memory_space=pltpu.SMEM)
    anyplace = pl.BlockSpec(memory_space=pl.ANY)
    whole = pl.pallas_call(
        lambda *refs: step(scale, *refs),
        out_shape=jax.ShapeDtypeStruct((NY, NL, 8, 640), F32),
        in_specs=[anyplace] * 7 + [smem],
        out_specs=vmem,
        scratch_shapes=[
            pltpu.VMEM((512, 1024), BF16),
            pltpu.VMEM((1024, 1024), BF16),
            pltpu.VMEM((1024, 256), BF16),
            pltpu.VMEM((16, 128), jnp.int32),
            pltpu.VMEM((15, 512), jnp.int32),
            pltpu.VMEM((1, 512), jnp.int32),
            pltpu.VMEM((15, 512), jnp.int32),
            pltpu.SemaphoreType.DMA((10,)),
            pltpu.VMEM((2, 8, 128, 512), BF16),
            pltpu.VMEM((512, 256), BF16),
            pltpu.VMEM((512, 1024), BF16),
            pltpu.VMEM((512, 256), F32),
            pltpu.VMEM((512, 256), BF16),
            pltpu.VMEM((512, 256), BF16),
            pltpu.VMEM((4, 512, 256), BF16),
            pltpu.VMEM((8, 8, 128), jnp.int32),
            pltpu.VMEM((8, 8, 128), jnp.int32),
            pltpu.VMEM((128, 512), F32),
            pltpu.VMEM((2, 7, 128, 256), BF16),
            pltpu.VMEM((4, 512, 256), BF16),
            pltpu.VMEM((4, 512, 512), BF16),
            pltpu.VMEM((512, 128), F32),
            pltpu.VMEM((1024, 512), BF16),
            pltpu.VMEM((1024, 512), BF16),
            pltpu.VMEM((512, 128), F32),
            pltpu.VMEM((512, 256), F32),
            pltpu.VMEM((512, 512), F32),
            pltpu.VMEM((512, 512), BF16),
            pltpu.VMEM((512, 1024), BF16),
            pltpu.VMEM((512, 256), BF16),
            pltpu.VMEM((1024, 640), F32),
            pltpu.VMEM((1024, 640), F32),
            pltpu.VMEM((4, 2, 4, 16, 640), BF16),
            pltpu.VMEM((4, 2, 4, 16, 640), BF16),
            pltpu.VMEM((4, 4, 2, 16, 640), BF16),
            pltpu.VMEM((4, 4, 2, 16, 640), BF16),
            pltpu.VMEM((4, 2, 4, 16, 640), BF16),
            pltpu.VMEM((3, 2, 4, 16, 640), BF16),
            pltpu.VMEM((4, 4, 2, 16, 640), BF16),
            pltpu.VMEM((3, 4, 2, 16, 640), BF16),
            pltpu.VMEM((4, 2, 16, 640), F32),
            pltpu.VMEM((4, 2, 16, 640), F32),
            pltpu.VMEM((4, 2, 16, 640), BF16),
            pltpu.VMEM((3, 2, 16, 640), BF16),
            pltpu.VMEM((4, 2, 16, 640), BF16),
            pltpu.VMEM((3, 2, 16, 640), BF16),
            pltpu.VMEM((2, 4, 8, 640), F32),
            pltpu.VMEM((8, 8, 640), F32),
            pltpu.VMEM((4, 4, 8, 640), F32),
            pltpu.SemaphoreType.DMA((80,)),
            pltpu.SemaphoreType.DMA((80,)),
        ],
        compiler_params=pltpu.CompilerParams(
            collective_id=0, has_side_effects=True, vmem_limit_bytes=56 << 20
        ),
        cost_estimate=pl.CostEstimate(flops=9_000_000_000, bytes_accessed=5_000_000, transcendentals=0),
        name="embedding_step",
    )(
        inputs, w_first, w_second, requests, slots.T, counts.reshape(1, -1), edge_weight.T, offsets
    )
    return pl.pallas_call(
        assemble,
        out_shape=(jax.ShapeDtypeStruct((64, 1024), F32), jax.ShapeDtypeStruct((64, 256), F32)),
        in_specs=[vmem],
        out_specs=(vmem, vmem),
        name="assemble",
    )(whole)


def solution(mesh):
    return jax.shard_map(
        shards,
        mesh=mesh,
        in_specs=(
            P(("wide", "narrow"), None),
            P(),
            P(),
            P(("wide", "narrow"), None),
            P(("wide", "narrow"), None),
            P(("wide", "narrow")),
            P(("wide", "narrow"), None),
            P(),
        ),
        out_specs=(P("wide", None), P("wide", None)),
        check_vma=False,
    )
```

```python
import math

import jax
import jax.numpy as jnp
from jax import lax
from jax.experimental import pallas as pl
from jax.experimental.pallas import tpu as pltpu
from jax.sharding import PartitionSpec as P

MESH = pl.DeviceIdType.MESH
F32 = jnp.float32
BF16 = jnp.bfloat16
NEGW = 8
NX, NH, NC, NL, NY = 4, 2, 2, 4, 4


def nt(a, b):
    return lax.dot_general(a, b, (((1,), (1,)), ((), ())), preferred_element_type=F32)


def nn(a, b):
    return jnp.dot(a, b, preferred_element_type=F32)


def step(
    scale, inputs_hbm, w1_hbm, w2_hbm, requests_hbm, slots_hbm, counts_hbm, edges_hbm, offsets, out0, out1,
    inputs, w1, w2, requests, slots, counts, edges, in_sem, picks, sent_part, hidden, codes, sent, mate, far, reqs, asked, keys, found, table, weights, norms,
    xt, ht, sums, acc, dist, coef, dpre, dcodes, asks_f, wishes, send_sem, recv_sem, *pairs,
):
    pair0, pair1 = pairs[:19], pairs[19:]
    w = lax.axis_index("wide")
    n = lax.axis_index("narrow")
    x, h, c = w // 4, (w // 2) % 2, w % 2
    l, y = n // 4, n % 4
    rows = inputs.shape[0]
    sem_count = [0]

    loads = []

    def load(src, dst):
        cp = pltpu.make_async_copy(src, dst, in_sem.at[len(loads)])
        cp.start()
        loads.append(cp)
        return cp

    need_requests = load(requests_hbm, requests)
    need_w1 = [load(w1_hbm.at[q : q + 256], w1.at[q : q + 256]) for q in range(0, 1024, 256)]
    need_inputs = [load(inputs_hbm.at[q : q + 128], inputs.at[q : q + 128]) for q in range(0, rows, 128)]
    need_w2 = load(w2_hbm, w2)

    def device(xx, hh, cc, ll, yy):
        return (xx * 4 + hh * 2 + cc, ll * 4 + yy)

    def copy(src, dst, target):
        at = sem_count[0]
        sem_count[0] += 1
        return pltpu.make_async_remote_copy(
            src_ref=src, dst_ref=dst, send_sem=send_sem.at[at], recv_sem=recv_sem.at[at],
            device_id=target, device_id_type=MESH,
        )

    def xs(s):
        return (x + s) % NX

    def ys(s):
        return (y + s) % NY

    def ls(s):
        return (l + s) % NL

    barrier = pltpu.get_barrier_semaphore()
    plane = [(dx, dc) for dx in range(NX) for dc in range(NC) if dx or dc]
    ring = [(dl, dy) for dl in range(NL) for dy in range(NY) if dl or dy]
    peers = [device(xs(dx), h, (c + dc) % 2, l, y) for dx, dc in plane]
    peers += [device(x, h, c, ls(dl), ys(dy)) for dl, dy in ring]
    peers += [device(x, 1 - h, c, ls(dl), y) for dl in range(NL)]
    for peer in peers:
        pl.semaphore_signal(barrier, inc=1, device_id=peer, device_id_type=MESH)

    need_requests.wait()
    reqs[...] = jnp.zeros_like(reqs)
    for xx in range(NX):
        for cc in range(NC):
            for hh in range(NH):
                p = xx * 4 + hh * 2 + cc
                reqs[xx * 2 + cc, hh : hh + 1, :] = requests[p : p + 1, :]

    for cp in need_w1:
        cp.wait()
    for q in range(4):
        need_inputs[q].wait()
        for at in range(0, 1024, 256):
            pre = nn(inputs[q * 128 : q * 128 + 128, :], w1[:, at : at + 256])
            hidden[q * 128 : q * 128 + 128, at : at + 256] = jnp.maximum(pre, 0.0).astype(BF16)
        if q == 0:
            lists = [load(slots_hbm, slots), load(counts_hbm, counts), load(edges_hbm, edges)]
    need_w2.wait()
    codes[...] = nn(hidden[...], w2[...])
    sent[...] = codes[...].astype(BF16)
    sent_part[...] = sent[...] * (2.0 / 256.0)

    pl.semaphore_wait(barrier, len(peers))

    ask = []
    for dx, dc in plane:
        j = dx * 2 + dc
        cp = copy(reqs.at[xs(dx) * 2 + (c + dc) % 2], asked.at[j], device(xs(dx), h, (c + dc) % 2, l, y))
        cp.start()
        ask.append(cp)
    to_next = copy(sent, far.at[3], device(x, h, c, ls(1), y))
    to_next.start()
    to_mate = []
    for e in range(2):
        cols = slice(e * 128, e * 128 + 128)
        cp = copy(sent.at[:, cols], mate.at[:, cols], device(x, 1 - h, c, l, y))
        cp.start()
        to_mate.append(cp)
    to_y = []
    for s in (1, 2, 3):
        cp = copy(sent, far.at[s - 1], device(x, h, c, l, ys(s)))
        to_y.append(cp)
        pl.when(y + s < NY)(cp.start)

    for cp in lists:
        cp.wait()
    live = lax.broadcasted_iota(jnp.int32, slots.shape, 0) < counts[...]
    keys[...] = jnp.zeros_like(keys)
    place = ((slots[...] - x * 512) & 2047) ^ (h * 256 + c * 128)
    keys[0:15, :] = place.astype(F32)
    keys[16:31, :] = jnp.where(live, edges[...], 0).astype(F32)
    norms[...] = keys[...].T

    def weigh(at, _):
        r = pl.multiple_of(at * 16, 16)
        both = norms[pl.ds(r, 16), :]
        lane = lax.broadcasted_iota(jnp.int32, (16, 512), 1).astype(F32)
        spots = [jnp.broadcast_to(both[:, k : k + 1], (16, 512)) for k in range(15)]
        worth = [jnp.broadcast_to(both[:, 16 + k : 17 + k], (16, 512)) for k in range(15)]
        for part in range(4):
            total = jnp.zeros((16, 512), F32)
            for k in range(15):
                total = total + jnp.where(spots[k] == lane + float(part * 512), worth[k], 0.0)
            weights[part, pl.ds(r, 16), :] = total.astype(BF16)
        return 0

    for cp in ask:
        cp.wait_recv()
    asked[0] = reqs[x * 2 + c]
    for j in range(8):
        norms2 = asked[j]
        asks_f[j * 8 : j * 8 + 8, :] = norms2.astype(F32)
    wishes[...] = asks_f[...].T

    lane = lax.broadcasted_iota(jnp.int32, (128, rows), 1).astype(F32)
    reply = {}

    def deliver(block, b, j, e):
        cols = slice(0, 256) if e is None else slice(e * 128, e * 128 + 128)
        got = nn(picks[b, j], block[:, cols]).astype(BF16)
        dx, dc = j // 2, j % 2
        spot = slice(b * 256 + dc * 128, b * 256 + dc * 128 + 128)
        if j == 0:
            table[0, spot, cols] = got
        else:
            found[b, j - 1, :, cols] = got
            cp = copy(
                found.at[b, j - 1, :, cols], table.at[dx, spot, cols],
                device(xs(NX - dx), h, (c + dc) % 2, l, y),
            )
            cp.start()
            reply.setdefault((b, dx), []).append(cp)

    turns = (2, 6, 4, 3, 7, 5, 1, 0)
    def choose(b):
        for j in turns:
            which = jnp.where((h + b) % 2 == 0, wishes[:, j * 8 : j * 8 + 1], wishes[:, j * 8 + 1 : j * 8 + 2])
            picks[b, j] = jnp.where(jnp.broadcast_to(which, (128, rows)) == lane, 1.0, 0.0).astype(BF16)
            if b == 0:
                deliver(sent, 0, j, None)

    choose(0)
    lax.fori_loop(0, rows // 32, weigh, 0)
    to_next.wait_recv()
    for s in (1, 2, 3):
        cp = pltpu.make_async_remote_copy(
            src_ref=far.at[3], dst_ref=far.at[s - 1], send_sem=send_sem.at[10 + s - 1],
            recv_sem=recv_sem.at[10 + s - 1], device_id=device(x, h, c, l, ys(s)), device_id_type=MESH,
        )
        pl.when(y + s >= NY)(cp.start)
    lax.fori_loop(rows // 32, rows // 16, weigh, 0)
    choose(1)
    for g in range(8):
        xt[g * 128 : g * 128 + 128, :] = inputs[:, g * 128 : g * 128 + 128].T
        ht[g * 128 : g * 128 + 128, :] = hidden[:, g * 128 : g * 128 + 128].T

    inv = 1.0 / 256.0
    own = sent[...].astype(F32)
    norm = jnp.sum(own * own, axis=1, keepdims=True)
    norms[...] = jnp.broadcast_to(norm * inv + 1.0, norms.shape)
    sums[...] = jnp.zeros_like(sums)
    acc[...] = jnp.zeros_like(acc)
    ones = jnp.ones((8, 256), BF16)

    def squares(block):
        z = block.astype(F32)
        z = z * z
        hi = z.astype(BF16)
        lo = (z - hi.astype(F32)).astype(BF16)
        return (nt(ones, hi) + nt(ones, lo))[0:1, :] * inv

    def pull(block, dx, b, offset):
        wide = block.shape[0]
        dist[:, 0:wide] = nt(sent_part[...], block[...])
        size = squares(block[...])

        def tile(at, _):
            r = pl.multiple_of(at * 64, 64)
            mine = norms[pl.ds(r, 64), :]
            total = sums[pl.ds(r, 64), :]
            for q in range(wide // 128):
                cols = slice(q * 128, q * 128 + 128)
                d = jnp.maximum((mine + size[:, cols]) - dist[pl.ds(r, 64), cols], 1.0)
                if dx is not None:
                    at_b = slice(b * 256 + q * 128, b * 256 + q * 128 + 128)
                    k = weights[dx, pl.ds(r, 64), at_b].astype(F32) * (1.0 / d)
                else:
                    i = lax.broadcasted_iota(jnp.int32, (64, 128), 0)
                    j = lax.broadcasted_iota(jnp.int32, (64, 128), 1)
                    band = ((j - i) + (q * 128 - r - offset)) & (rows - 1)
                    k = jnp.where(band < NEGW, -1.0 / (d * (1.1 * (d - 1.0) + 0.1)), 0.0)
                k = k.astype(BF16)
                coef[pl.ds(r, 64), cols] = k
                total = total + k.astype(F32)
            sums[pl.ds(r, 64), :] = total
            return 0

        lax.fori_loop(0, rows // 64, tile, 0)
        acc[...] += nn(coef[:, 0:wide], block[...])

    def attract(b):
        for dx in (0, 1, 3, 2):
            for cp in reply[b, dx]:
                cp.wait_recv()
            pull(table.at[dx, b * 256 : b * 256 + 256], dx, b, None)

    attract(0)
    for e in range(2):
        to_mate[e].wait_recv()
        for j in turns:
            deliver(mate, 1, j, e)
    pull(far.at[3], None, None, offsets[3])
    for s in (1, 3, 2):
        to_y[s - 1].wait_recv()
        pull(far.at[s - 1], None, None, offsets[s - 1])
    attract(1)

    total = jnp.sum(sums[...], axis=1, keepdims=True)
    dcodes[...] = (scale * (total * codes[...] - acc[...])).astype(BF16)

    core = device(x, h, 1 - c, l, y)

    def backward(g, first, width):
        for at in range(first, first + width, 128):
            back = nt(dcodes[...], w2[at : at + 128, :])
            dpre[:, at : at + 128] = jnp.where(hidden[:, at : at + 128] > 0, back, 0.0).astype(BF16)
        g[...] = nn(xt[...], dpre[:, first : first + width])

    def part_rows(xx, hh, cc, yy):
        return pl.ds(pl.multiple_of(xx * 256 + hh * 128 + cc * 64 + yy * 16, 16), 16)

    each = [(xx, hh, yy) for xx in range(NX) for hh in range(NH) for yy in range(NY)]
    sends = []

    def go(src, dst, target):
        cp = copy(src, dst, target)
        cp.start()
        sends.append(cp)
        return cp

    def spot(kind, xx, hh, yy):
        return (xx, hh, yy) if kind == "a" else (yy, hh, xx)

    class Chunk:
        def __init__(self, kind, g, c_out, c_in, p_out, p_in, f, q_out, q_in):
            self.kind, self.g, self.c_out, self.c_in, self.p_out, self.p_in = kind, g, c_out, c_in, p_out, p_in
            self.f, self.q_out, self.q_in = f, q_out, q_in

        def near(self, s):
            return (xs(s), device(xs(s), h, c, l, y)) if self.kind == "a" else (ys(s), device(x, h, c, l, ys(s)))

        def beyond(self, s):
            return (ys(s), device(x, h, c, l, ys(s))) if self.kind == "a" else (xs(s), device(xs(s), h, c, l, y))

        def to_core(self):
            for xx, hh, yy in each:
                self.c_out[spot(self.kind, xx, hh, yy)] = self.g[part_rows(xx, hh, 1 - c, yy), :].astype(BF16)
            self.core = go(self.c_out, self.c_in, core)

        def first(self):
            self.core.wait_recv()
            for xx, hh, yy in each:
                at = spot(self.kind, xx, hh, yy)
                self.p_out[at] = (self.g[part_rows(xx, hh, c, yy), :] + self.c_in[at].astype(F32)).astype(BF16)
            self.one = []
            for s in (2, 1, 3):
                at, target = self.near(s)
                self.one.append(go(self.p_out.at[at], self.p_in.at[s - 1], target))
            mine = x if self.kind == "a" else y
            for far_at in range(4):
                for hh in range(NH):
                    rows_at = part_rows(x, hh, c, far_at) if self.kind == "a" else part_rows(far_at, hh, c, y)
                    self.f[hh, far_at] = self.g[rows_at, :] + self.c_in[mine, hh, far_at].astype(F32)

        def second(self):
            for cp in self.one:
                cp.wait_recv()
            for hh in range(NH):
                for far_at in range(4):
                    got = [self.p_in[s, hh, far_at].astype(F32) for s in range(3)]
                    self.f[hh, far_at] += got[0] + got[1] + got[2]
                    self.q_out[far_at, hh] = self.f[hh, far_at].astype(BF16)
            self.two = []
            for s in (2, 1, 3):
                at, target = self.beyond(s)
                self.two.append(go(self.q_out.at[at], self.q_in.at[s - 1], target))

        def result(self, hh):
            mine = y if self.kind == "a" else x
            got = [self.q_in[s, hh].astype(F32) for s in range(3)]
            return self.f[hh, mine] + got[0] + got[1] + got[2]

    class Pair:
        def __init__(self, a, b, zs_out, zs_in, whole):
            self.a, self.b, self.zs_out, self.zs_in, self.whole = a, b, zs_out, zs_in, whole

        def over_z(self):
            for cp in self.a.two + self.b.two:
                cp.wait_recv()
            for hh in range(NH):
                for half, chunk in enumerate((self.a, self.b)):
                    total = chunk.result(hh)
                    self.zs_out[hh, half] = total[0:8, :]
                    self.zs_out[hh, 2 + half] = total[8:16, :]
            self.zs = []
            for dh, dl in ((1, 0), (1, 2), (1, 1), (1, 3), (0, 2), (0, 1), (0, 3)):
                hh = (h + dh) % 2
                self.zs.append(
                    go(self.zs_out.at[hh, ls(dl)], self.zs_in.at[dh * 4 + dl], device(x, hh, c, ls(dl), y))
                )

        def spread(self):
            total = self.zs_out[h, l]
            for cp in self.zs:
                cp.wait_recv()
            for k in range(1, 8):
                total = total + self.zs_in[k]
            self.whole[y, l] = total
            self.last = [
                go(self.whole.at[y, l], self.whole.at[y, l], device(x, h, c, ls(dl), ys(dy)))
                for dl, dy in ring
            ]

    a0, b0 = Chunk("a", *pair0[0:8]), Chunk("b", *pair0[8:16])
    a1, b1 = Chunk("a", *pair1[0:8]), Chunk("b", *pair1[8:16])
    p0, p1 = Pair(a0, b0, *pair0[16:19]), Pair(a1, b1, *pair1[16:19])
    backward(b0.g, 0, 384)
    b0.to_core()
    backward(a0.g, 384, 384)
    a0.to_core()
    b0.first()
    a0.first()
    a1.g[...] = nn(ht[...], dcodes[...])
    a1.to_core()
    backward(b1.g, 768, 256)
    b1.to_core()
    a1.first()
    b1.first()
    b0.second()
    a0.second()
    a1.second()
    b1.second()
    p0.over_z()
    p1.over_z()
    p0.spread()
    p1.spread()
    for cp in p0.last:
        cp.wait_recv()
    out0[...] = p0.whole[...]
    for cp in p1.last:
        cp.wait_recv()
    out1[...] = p1.whole[...]

    for cp in ask + [to_next] + to_mate + to_y + sum(reply.values(), []) + sends:
        cp.wait_send()


def pair_scratch(width):
    chunk = [
        pltpu.VMEM((1024, width), F32),
        pltpu.VMEM((4, 2, 4, 16, width), BF16),
        pltpu.VMEM((4, 2, 4, 16, width), BF16),
        pltpu.VMEM((4, 2, 4, 16, width), BF16),
        pltpu.VMEM((3, 2, 4, 16, width), BF16),
        pltpu.VMEM((2, 4, 16, width), F32),
        pltpu.VMEM((4, 2, 16, width), BF16),
        pltpu.VMEM((3, 2, 16, width), BF16),
    ]
    shared = [
        pltpu.VMEM((2, 4, 8, width), F32),
        pltpu.VMEM((8, 8, width), F32),
        pltpu.VMEM((4, 4, 8, width), F32),
    ]
    return chunk + chunk + shared


def assemble(whole0, whole1, out_first, out_second):
    for yy in range(NY):
        for ll in range(NL):
            at = slice(yy * 16 + (ll // 2) * 8, yy * 16 + (ll // 2) * 8 + 8)
            if ll % 2 == 0:
                out_first[at, 384:768] = whole0[yy, ll]
                out_second[at, :] = whole1[yy, ll]
            else:
                out_first[at, 0:384] = whole0[yy, ll]
                out_first[at, 768:1024] = whole1[yy, ll]


def shards(inputs, w_first, w_second, requests, slots, counts, edge_weight, offsets):
    rows = inputs.shape[0]
    total_rows = rows * lax.axis_size("wide") * lax.axis_size("narrow")
    scale = 2.0 / (slots.shape[1] * math.sqrt(total_rows))
    vmem = pl.BlockSpec(memory_space=pltpu.VMEM)
    smem = pl.BlockSpec(memory_space=pltpu.SMEM)
    anyplace = pl.BlockSpec(memory_space=pl.ANY)
    whole0, whole1 = pl.pallas_call(
        lambda *refs: step(scale, *refs),
        out_shape=(
            jax.ShapeDtypeStruct((NY, NL, 8, 384), F32),
            jax.ShapeDtypeStruct((NY, NL, 8, 256), F32),
        ),
        in_specs=[anyplace] * 7 + [smem],
        out_specs=(vmem, vmem),
        scratch_shapes=[
            pltpu.VMEM((512, 1024), BF16),
            pltpu.VMEM((1024, 1024), BF16),
            pltpu.VMEM((1024, 256), BF16),
            pltpu.VMEM((16, 128), jnp.int32),
            pltpu.VMEM((15, 512), jnp.int32),
            pltpu.VMEM((1, 512), jnp.int32),
            pltpu.VMEM((15, 512), jnp.int32),
            pltpu.SemaphoreType.DMA((16,)),
            pltpu.VMEM((2, 8, 128, 512), BF16),
            pltpu.VMEM((512, 256), BF16),
            pltpu.VMEM((512, 1024), BF16),
            pltpu.VMEM((512, 256), F32),
            pltpu.VMEM((512, 256), BF16),
            pltpu.VMEM((512, 256), BF16),
            pltpu.VMEM((4, 512, 256), BF16),
            pltpu.VMEM((8, 8, 128), jnp.int32),
            pltpu.VMEM((8, 8, 128), jnp.int32),
            pltpu.VMEM((128, 512), F32),
            pltpu.VMEM((2, 7, 128, 256), BF16),
            pltpu.VMEM((4, 512, 256), BF16),
            pltpu.VMEM((4, 512, 512), BF16),
            pltpu.VMEM((512, 128), F32),
            pltpu.VMEM((1024, 512), BF16),
            pltpu.VMEM((1024, 512), BF16),
            pltpu.VMEM((512, 128), F32),
            pltpu.VMEM((512, 256), F32),
            pltpu.VMEM((512, 512), F32),
            pltpu.VMEM((512, 512), BF16),
            pltpu.VMEM((512, 1024), BF16),
            pltpu.VMEM((512, 256), BF16),
            pltpu.VMEM((128, 128), F32),
            pltpu.VMEM((128, 128), F32),
            pltpu.SemaphoreType.DMA((128,)),
            pltpu.SemaphoreType.DMA((128,)),
        ]
        + pair_scratch(384)
        + pair_scratch(256),
        compiler_params=pltpu.CompilerParams(
            collective_id=0, has_side_effects=True, vmem_limit_bytes=56 << 20
        ),
        cost_estimate=pl.CostEstimate(flops=9_000_000_000, bytes_accessed=5_000_000, transcendentals=0),
        name="embedding_step",
    )(
        inputs, w_first, w_second, requests, slots.T, counts.reshape(1, -1), edge_weight.T, offsets
    )
    return pl.pallas_call(
        assemble,
        out_shape=(jax.ShapeDtypeStruct((64, 1024), F32), jax.ShapeDtypeStruct((64, 256), F32)),
        in_specs=[vmem, vmem],
        out_specs=(vmem, vmem),
        name="assemble",
    )(whole0, whole1)


def solution(mesh):
    return jax.shard_map(
        shards,
        mesh=mesh,
        in_specs=(
            P(("wide", "narrow"), None),
            P(),
            P(),
            P(("wide", "narrow"), None),
            P(("wide", "narrow"), None),
            P(("wide", "narrow")),
            P(("wide", "narrow"), None),
            P(),
        ),
        out_specs=(P("wide", None), P("wide", None)),
        check_vma=False,
    )
```

```python
import math

import jax
import jax.numpy as jnp
from jax import lax
from jax.experimental import pallas as pl
from jax.experimental.pallas import tpu as pltpu
from jax.sharding import PartitionSpec as P

MESH = pl.DeviceIdType.MESH
F32 = jnp.float32
BF16 = jnp.bfloat16
NEGW = 8
NX, NH, NC, NL, NY = 4, 2, 2, 4, 4


def nt(a, b):
    return lax.dot_general(a, b, (((1,), (1,)), ((), ())), preferred_element_type=F32)


def nn(a, b):
    return jnp.dot(a, b, preferred_element_type=F32)


def step(
    scale, inputs_hbm, w1_hbm, w2_hbm, requests_hbm, slots_hbm, counts_hbm, edges_hbm, offsets, out0, out1,
    inputs, w1, w2, requests, slots, counts, edges, in_sem, picks, sent_part, hidden, codes, sent, mate, far, reqs, asked, keys, found, table, weights, norms,
    xt, ht, sums, acc, dist, coef, dpre, dcodes, asks_f, wishes, send_sem, recv_sem, *pairs,
):
    pair0, pair1 = pairs[:19], pairs[19:]
    w = lax.axis_index("wide")
    n = lax.axis_index("narrow")
    x, h, c = w // 4, (w // 2) % 2, w % 2
    l, y = n // 4, n % 4
    rows = inputs.shape[0]
    sem_count = [0]

    loads = []

    def load(src, dst):
        cp = pltpu.make_async_copy(src, dst, in_sem.at[len(loads)])
        cp.start()
        loads.append(cp)
        return cp

    lists = [load(slots_hbm, slots), load(counts_hbm, counts), load(edges_hbm, edges)]
    need_requests = load(requests_hbm, requests)
    need_w1 = [load(w1_hbm.at[q : q + 256], w1.at[q : q + 256]) for q in range(0, 1024, 256)]
    need_inputs = [load(inputs_hbm.at[q : q + 128], inputs.at[q : q + 128]) for q in range(0, rows, 128)]
    need_w2 = load(w2_hbm, w2)

    def device(xx, hh, cc, ll, yy):
        return (xx * 4 + hh * 2 + cc, ll * 4 + yy)

    def copy(src, dst, target):
        at = sem_count[0]
        sem_count[0] += 1
        return pltpu.make_async_remote_copy(
            src_ref=src, dst_ref=dst, send_sem=send_sem.at[at], recv_sem=recv_sem.at[at],
            device_id=target, device_id_type=MESH,
        )

    def xs(s):
        return (x + s) % NX

    def ys(s):
        return (y + s) % NY

    def ls(s):
        return (l + s) % NL

    barrier = pltpu.get_barrier_semaphore()
    plane = [(dx, dc) for dx in range(NX) for dc in range(NC) if dx or dc]
    ring = [(dl, dy) for dl in range(NL) for dy in range(NY) if dl or dy]
    peers = [device(xs(dx), h, (c + dc) % 2, l, y) for dx, dc in plane]
    peers += [device(x, h, c, ls(dl), ys(dy)) for dl, dy in ring]
    peers += [device(x, 1 - h, c, ls(dl), y) for dl in range(NL)]
    for peer in peers:
        pl.semaphore_signal(barrier, inc=1, device_id=peer, device_id_type=MESH)

    need_requests.wait()
    reqs[...] = jnp.zeros_like(reqs)
    for xx in range(NX):
        for cc in range(NC):
            for hh in range(NH):
                p = xx * 4 + hh * 2 + cc
                reqs[xx * 2 + cc, hh : hh + 1, :] = requests[p : p + 1, :]

    for cp in lists:
        cp.wait()
    live = lax.broadcasted_iota(jnp.int32, slots.shape, 0) < counts[...]
    place = ((slots[...] - x * 512) & 2047) ^ (h * 256 + c * 128)
    worth = jnp.where(live, edges[...], 0) << (((place >> 7) & 3) * 8)
    keys[...] = jnp.zeros_like(keys)
    keys[0:15, :] = (((place >> 9) << 7) | (place & 127)).astype(F32)
    keys[16:31, :] = worth.astype(F32)
    norms[...] = keys[...].T

    def weigh(at, _):
        r = pl.multiple_of(at * 16, 16)
        both = norms[pl.ds(r, 16), :].astype(jnp.int32)
        lane = lax.broadcasted_iota(jnp.int32, (16, 128), 1)
        total = [jnp.zeros((16, 128), jnp.int32) for _ in range(4)]
        for k in range(15):
            spot = jnp.broadcast_to(both[:, k : k + 1], (16, 128))
            value = jnp.broadcast_to(both[:, 16 + k : 17 + k], (16, 128))
            for part in range(4):
                total[part] = total[part] + jnp.where(spot == lane + part * 128, value, 0)
        for part in range(4):
            weights[part, pl.ds(r, 16), :] = total[part]
        return 0

    lax.fori_loop(0, rows // 32, weigh, 0)

    for cp in need_w1:
        cp.wait()
    for q in range(4):
        need_inputs[q].wait()
        for at in range(0, 1024, 256):
            pre = nn(inputs[q * 128 : q * 128 + 128, :], w1[:, at : at + 256])
            hidden[q * 128 : q * 128 + 128, at : at + 256] = jnp.maximum(pre, 0.0).astype(BF16)
    need_w2.wait()
    codes[...] = nn(hidden[...], w2[...])
    sent[...] = codes[...].astype(BF16)
    sent_part[...] = sent[...] * (2.0 / 256.0)

    pl.semaphore_wait(barrier, len(peers))

    ask = []
    for dx, dc in plane:
        j = dx * 2 + dc
        cp = copy(reqs.at[xs(dx) * 2 + (c + dc) % 2], asked.at[j], device(xs(dx), h, (c + dc) % 2, l, y))
        cp.start()
        ask.append(cp)
    to_next = copy(sent, far.at[3], device(x, h, c, ls(1), y))
    to_next.start()
    to_mate = []
    for e in range(2):
        cols = slice(e * 128, e * 128 + 128)
        cp = copy(sent.at[:, cols], mate.at[:, cols], device(x, 1 - h, c, l, y))
        cp.start()
        to_mate.append(cp)
    to_y = []
    for s in (1, 2, 3):
        cp = copy(sent, far.at[s - 1], device(x, h, c, l, ys(s)))
        to_y.append(cp)
        pl.when(y + s < NY)(cp.start)

    for g in range(8):
        xt[g * 128 : g * 128 + 128, :] = inputs[:, g * 128 : g * 128 + 128].T
    for cp in ask:
        cp.wait_recv()
    asked[0] = reqs[x * 2 + c]
    for j in range(8):
        norms2 = asked[j]
        asks_f[j * 8 : j * 8 + 8, :] = norms2.astype(F32)
    wishes[...] = asks_f[...].T

    lane = lax.broadcasted_iota(jnp.int32, (128, rows), 1).astype(F32)
    reply = {}

    def deliver(block, b, j, e):
        cols = slice(0, 256) if e is None else slice(e * 128, e * 128 + 128)
        got = nn(picks[b, j], block[:, cols]).astype(BF16)
        dx, dc = j // 2, j % 2
        spot = slice(b * 256 + dc * 128, b * 256 + dc * 128 + 128)
        if j == 0:
            table[0, spot, cols] = got
        else:
            found[b, j - 1, :, cols] = got
            cp = copy(
                found.at[b, j - 1, :, cols], table.at[dx, spot, cols],
                device(xs(NX - dx), h, (c + dc) % 2, l, y),
            )
            cp.start()
            reply.setdefault((b, dx), []).append(cp)

    turns = (2, 6, 4, 3, 7, 5, 1, 0)
    def choose(b):
        for j in turns:
            which = jnp.where((h + b) % 2 == 0, wishes[:, j * 8 : j * 8 + 1], wishes[:, j * 8 + 1 : j * 8 + 2])
            picks[b, j] = jnp.where(jnp.broadcast_to(which, (128, rows)) == lane, 1.0, 0.0).astype(BF16)
            if b == 0:
                deliver(sent, 0, j, None)

    choose(0)
    lax.fori_loop(rows // 32, rows // 16, weigh, 0)
    to_next.wait_recv()
    for s in (1, 2, 3):
        cp = pltpu.make_async_remote_copy(
            src_ref=far.at[3], dst_ref=far.at[s - 1], send_sem=send_sem.at[10 + s - 1],
            recv_sem=recv_sem.at[10 + s - 1], device_id=device(x, h, c, l, ys(s)), device_id_type=MESH,
        )
        pl.when(y + s >= NY)(cp.start)
    choose(1)
    for g in range(8):
        ht[g * 128 : g * 128 + 128, :] = hidden[:, g * 128 : g * 128 + 128].T

    inv = 1.0 / 256.0
    own = sent[...].astype(F32)
    norm = jnp.sum(own * own, axis=1, keepdims=True)
    norms[...] = jnp.broadcast_to(norm * inv + 1.0, norms.shape)
    sums[...] = jnp.zeros_like(sums)
    acc[...] = jnp.zeros_like(acc)
    ones = jnp.ones((8, 256), BF16)

    def squares(block):
        z = block.astype(F32)
        z = z * z
        hi = z.astype(BF16)
        lo = (z - hi.astype(F32)).astype(BF16)
        return (nt(ones, hi) + nt(ones, lo))[0:1, :] * inv

    def pull(block, dx, b, offset):
        wide = block.shape[0]
        dist[:, 0:wide] = nt(sent_part[...], block[...])
        size = squares(block[...])

        def tile(at, _):
            r = pl.multiple_of(at * 64, 64)
            mine = norms[pl.ds(r, 64), :]
            total = sums[pl.ds(r, 64), :]
            for q in range(wide // 128):
                cols = slice(q * 128, q * 128 + 128)
                d = jnp.maximum((mine + size[:, cols]) - dist[pl.ds(r, 64), cols], 1.0)
                if dx is not None:
                    count = (weights[dx, pl.ds(r, 64), :] >> (8 * (b * 2 + q))) & 255
                    k = count.astype(F32) * (1.0 / d)
                else:
                    i = lax.broadcasted_iota(jnp.int32, (64, 128), 0)
                    j = lax.broadcasted_iota(jnp.int32, (64, 128), 1)
                    band = ((j - i) + (q * 128 - r - offset)) & (rows - 1)
                    k = jnp.where(band < NEGW, -1.0 / (d * (1.1 * (d - 1.0) + 0.1)), 0.0)
                k = k.astype(BF16)
                coef[pl.ds(r, 64), cols] = k
                total = total + k.astype(F32)
            sums[pl.ds(r, 64), :] = total
            return 0

        lax.fori_loop(0, rows // 64, tile, 0)
        acc[...] += nn(coef[:, 0:wide], block[...])

    def attract(b):
        for dx in (0, 1, 3, 2):
            for cp in reply[b, dx]:
                cp.wait_recv()
            pull(table.at[dx, b * 256 : b * 256 + 256], dx, b, None)

    attract(0)
    for e in range(2):
        to_mate[e].wait_recv()
        for j in turns:
            deliver(mate, 1, j, e)
    pull(far.at[3], None, None, offsets[3])
    for s in (1, 3, 2):
        to_y[s - 1].wait_recv()
        pull(far.at[s - 1], None, None, offsets[s - 1])
    attract(1)

    total = jnp.sum(sums[...], axis=1, keepdims=True)
    dcodes[...] = (scale * (total * codes[...] - acc[...])).astype(BF16)

    core = device(x, h, 1 - c, l, y)

    def backward(g, first, width):
        for at in range(first, first + width, 128):
            back = nt(dcodes[...], w2[at : at + 128, :])
            dpre[:, at : at + 128] = jnp.where(hidden[:, at : at + 128] > 0, back, 0.0).astype(BF16)
        g[...] = nn(xt[...], dpre[:, first : first + width])

    def part_rows(xx, hh, cc, yy):
        return pl.ds(pl.multiple_of(xx * 256 + hh * 128 + cc * 64 + yy * 16, 16), 16)

    each = [(xx, hh, yy) for xx in range(NX) for hh in range(NH) for yy in range(NY)]
    sends = []

    def go(src, dst, target):
        cp = copy(src, dst, target)
        cp.start()
        sends.append(cp)
        return cp

    def spot(kind, xx, hh, yy):
        return (xx, hh, yy) if kind == "a" else (yy, hh, xx)

    class Chunk:
        def __init__(self, kind, g, c_out, c_in, p_out, p_in, f, q_out, q_in):
            self.kind, self.g, self.c_out, self.c_in, self.p_out, self.p_in = kind, g, c_out, c_in, p_out, p_in
            self.f, self.q_out, self.q_in = f, q_out, q_in

        def near(self, s):
            return (xs(s), device(xs(s), h, c, l, y)) if self.kind == "a" else (ys(s), device(x, h, c, l, ys(s)))

        def beyond(self, s):
            return (ys(s), device(x, h, c, l, ys(s))) if self.kind == "a" else (xs(s), device(xs(s), h, c, l, y))

        def to_core(self):
            for xx, hh, yy in each:
                self.c_out[spot(self.kind, xx, hh, yy)] = self.g[part_rows(xx, hh, 1 - c, yy), :].astype(BF16)
            self.core = go(self.c_out, self.c_in, core)

        def first(self):
            self.core.wait_recv()
            for xx, hh, yy in each:
                at = spot(self.kind, xx, hh, yy)
                self.p_out[at] = (self.g[part_rows(xx, hh, c, yy), :] + self.c_in[at].astype(F32)).astype(BF16)
            self.one = []
            for s in (2, 1, 3):
                at, target = self.near(s)
                self.one.append(go(self.p_out.at[at], self.p_in.at[s - 1], target))
            mine = x if self.kind == "a" else y
            for far_at in range(4):
                for hh in range(NH):
                    rows_at = part_rows(x, hh, c, far_at) if self.kind == "a" else part_rows(far_at, hh, c, y)
                    self.f[hh, far_at] = self.g[rows_at, :] + self.c_in[mine, hh, far_at].astype(F32)

        def second(self):
            for cp in self.one:
                cp.wait_recv()
            for hh in range(NH):
                for far_at in range(4):
                    got = [self.p_in[s, hh, far_at].astype(F32) for s in range(3)]
                    self.f[hh, far_at] += got[0] + got[1] + got[2]
                    self.q_out[far_at, hh] = self.f[hh, far_at].astype(BF16)
            self.two = []
            for s in (2, 1, 3):
                at, target = self.beyond(s)
                self.two.append(go(self.q_out.at[at], self.q_in.at[s - 1], target))

        def result(self, hh):
            mine = y if self.kind == "a" else x
            got = [self.q_in[s, hh].astype(F32) for s in range(3)]
            return self.f[hh, mine] + got[0] + got[1] + got[2]

    class Pair:
        def __init__(self, a, b, zs_out, zs_in, whole):
            self.a, self.b, self.zs_out, self.zs_in, self.whole = a, b, zs_out, zs_in, whole

        def over_z(self):
            for cp in self.a.two + self.b.two:
                cp.wait_recv()
            for hh in range(NH):
                for half, chunk in enumerate((self.a, self.b)):
                    total = chunk.result(hh)
                    self.zs_out[hh, half] = total[0:8, :]
                    self.zs_out[hh, 2 + half] = total[8:16, :]
            self.zs = []
            for dh, dl in ((1, 0), (1, 2), (1, 1), (1, 3), (0, 2), (0, 1), (0, 3)):
                hh = (h + dh) % 2
                self.zs.append(
                    go(self.zs_out.at[hh, ls(dl)], self.zs_in.at[dh * 4 + dl], device(x, hh, c, ls(dl), y))
                )

        def spread(self):
            total = self.zs_out[h, l]
            for cp in self.zs:
                cp.wait_recv()
            for k in range(1, 8):
                total = total + self.zs_in[k]
            self.whole[y, l] = total
            self.along = {}
            self.last = []
            for dl in (2, 1, 3):
                piece = self.whole.at[y, l]
                self.along[dl] = go(piece, piece, device(x, h, c, ls(dl), y))
            self.pass_on(l)

        def pass_on(self, ll):
            for s in (2, 1, 3):
                piece = self.whole.at[y, ll]
                self.last.append(go(piece, piece, device(x, h, c, l, ys(s))))

        def relay(self):
            for dl in (1, 3, 2):
                self.along[dl].wait_recv()
                self.pass_on(ls(NL - dl))

    a0, b0 = Chunk("a", *pair0[0:8]), Chunk("b", *pair0[8:16])
    a1, b1 = Chunk("a", *pair1[0:8]), Chunk("b", *pair1[8:16])
    p0, p1 = Pair(a0, b0, *pair0[16:19]), Pair(a1, b1, *pair1[16:19])
    backward(b0.g, 0, 384)
    b0.to_core()
    backward(a0.g, 384, 384)
    a0.to_core()
    b0.first()
    a0.first()
    a1.g[...] = nn(ht[...], dcodes[...])
    a1.to_core()
    backward(b1.g, 768, 256)
    b1.to_core()
    a1.first()
    b1.first()
    b0.second()
    a0.second()
    a1.second()
    b1.second()
    p0.over_z()
    p1.over_z()
    p0.spread()
    p1.spread()
    p0.relay()
    p1.relay()
    for cp in p0.last:
        cp.wait_recv()
    out0[...] = p0.whole[...]
    for cp in p1.last:
        cp.wait_recv()
    out1[...] = p1.whole[...]

    for cp in ask + [to_next] + to_mate + to_y + sum(reply.values(), []) + sends:
        cp.wait_send()


def pair_scratch(width):
    chunk = [
        pltpu.VMEM((1024, width), F32),
        pltpu.VMEM((4, 2, 4, 16, width), BF16),
        pltpu.VMEM((4, 2, 4, 16, width), BF16),
        pltpu.VMEM((4, 2, 4, 16, width), BF16),
        pltpu.VMEM((3, 2, 4, 16, width), BF16),
        pltpu.VMEM((2, 4, 16, width), F32),
        pltpu.VMEM((4, 2, 16, width), BF16),
        pltpu.VMEM((3, 2, 16, width), BF16),
    ]
    shared = [
        pltpu.VMEM((2, 4, 8, width), F32),
        pltpu.VMEM((8, 8, width), F32),
        pltpu.VMEM((4, 4, 8, width), F32),
    ]
    return chunk + chunk + shared


def assemble(whole0, whole1, out_first, out_second):
    for yy in range(NY):
        for ll in range(NL):
            at = slice(yy * 16 + (ll // 2) * 8, yy * 16 + (ll // 2) * 8 + 8)
            if ll % 2 == 0:
                out_first[at, 384:768] = whole0[yy, ll]
                out_second[at, :] = whole1[yy, ll]
            else:
                out_first[at, 0:384] = whole0[yy, ll]
                out_first[at, 768:1024] = whole1[yy, ll]


def shards(inputs, w_first, w_second, requests, slots, counts, edge_weight, offsets):
    rows = inputs.shape[0]
    total_rows = rows * lax.axis_size("wide") * lax.axis_size("narrow")
    scale = 2.0 / (slots.shape[1] * math.sqrt(total_rows))
    vmem = pl.BlockSpec(memory_space=pltpu.VMEM)
    smem = pl.BlockSpec(memory_space=pltpu.SMEM)
    anyplace = pl.BlockSpec(memory_space=pl.ANY)
    whole0, whole1 = pl.pallas_call(
        lambda *refs: step(scale, *refs),
        out_shape=(
            jax.ShapeDtypeStruct((NY, NL, 8, 384), F32),
            jax.ShapeDtypeStruct((NY, NL, 8, 256), F32),
        ),
        in_specs=[anyplace] * 7 + [smem],
        out_specs=(vmem, vmem),
        scratch_shapes=[
            pltpu.VMEM((512, 1024), BF16),
            pltpu.VMEM((1024, 1024), BF16),
            pltpu.VMEM((1024, 256), BF16),
            pltpu.VMEM((16, 128), jnp.int32),
            pltpu.VMEM((15, 512), jnp.int32),
            pltpu.VMEM((1, 512), jnp.int32),
            pltpu.VMEM((15, 512), jnp.int32),
            pltpu.SemaphoreType.DMA((16,)),
            pltpu.VMEM((2, 8, 128, 512), BF16),
            pltpu.VMEM((512, 256), BF16),
            pltpu.VMEM((512, 1024), BF16),
            pltpu.VMEM((512, 256), F32),
            pltpu.VMEM((512, 256), BF16),
            pltpu.VMEM((512, 256), BF16),
            pltpu.VMEM((4, 512, 256), BF16),
            pltpu.VMEM((8, 8, 128), jnp.int32),
            pltpu.VMEM((8, 8, 128), jnp.int32),
            pltpu.VMEM((128, 512), F32),
            pltpu.VMEM((2, 7, 128, 256), BF16),
            pltpu.VMEM((4, 512, 256), BF16),
            pltpu.VMEM((4, 512, 128), jnp.int32),
            pltpu.VMEM((512, 128), F32),
            pltpu.VMEM((1024, 512), BF16),
            pltpu.VMEM((1024, 512), BF16),
            pltpu.VMEM((512, 128), F32),
            pltpu.VMEM((512, 256), F32),
            pltpu.VMEM((512, 512), F32),
            pltpu.VMEM((512, 512), BF16),
            pltpu.VMEM((512, 1024), BF16),
            pltpu.VMEM((512, 256), BF16),
            pltpu.VMEM((128, 128), F32),
            pltpu.VMEM((128, 128), F32),
            pltpu.SemaphoreType.DMA((128,)),
            pltpu.SemaphoreType.DMA((128,)),
        ]
        + pair_scratch(384)
        + pair_scratch(256),
        compiler_params=pltpu.CompilerParams(
            collective_id=0, has_side_effects=True, vmem_limit_bytes=56 << 20
        ),
        cost_estimate=pl.CostEstimate(flops=9_000_000_000, bytes_accessed=5_000_000, transcendentals=0),
        name="embedding_step",
    )(
        inputs, w_first, w_second, requests, slots.T, counts.reshape(1, -1), edge_weight.T, offsets
    )
    return pl.pallas_call(
        assemble,
        out_shape=(jax.ShapeDtypeStruct((64, 1024), F32), jax.ShapeDtypeStruct((64, 256), F32)),
        in_specs=[vmem, vmem],
        out_specs=(vmem, vmem),
        name="assemble",
    )(whole0, whole1)


def solution(mesh):
    return jax.shard_map(
        shards,
        mesh=mesh,
        in_specs=(
            P(("wide", "narrow"), None),
            P(),
            P(),
            P(("wide", "narrow"), None),
            P(("wide", "narrow"), None),
            P(("wide", "narrow")),
            P(("wide", "narrow"), None),
            P(),
        ),
        out_specs=(P("wide", None), P("wide", None)),
        check_vma=False,
    )
```

```python
import math

import jax
import jax.numpy as jnp
from jax import lax
from jax.experimental import pallas as pl
from jax.experimental.pallas import tpu as pltpu
from jax.sharding import PartitionSpec as P

MESH = pl.DeviceIdType.MESH
F32 = jnp.float32
BF16 = jnp.bfloat16
NEGW = 8
NX, NH, NC, NL, NY = 4, 2, 2, 4, 4


def nt(a, b):
    return lax.dot_general(a, b, (((1,), (1,)), ((), ())), preferred_element_type=F32)


def nn(a, b):
    return jnp.dot(a, b, preferred_element_type=F32)


def step(
    scale, inputs_hbm, w1_hbm, w2_hbm, requests_hbm, slots_hbm, counts_hbm, edges_hbm, offsets, out0, out1,
    inputs, w1, w2, requests, slots, counts, edges, in_sem, picks, sent_part, hidden, codes, sent, mate, far, reqs, asked, keys, found, table, weights, norms,
    xt, ht, sums, acc, dist, coef, dpre, dcodes, asks_f, wishes, send_sem, recv_sem, *pairs,
):
    pair0, pair1 = pairs[:19], pairs[19:]
    w = lax.axis_index("wide")
    n = lax.axis_index("narrow")
    x, h, c = w // 4, (w // 2) % 2, w % 2
    l, y = n // 4, n % 4
    rows = inputs.shape[0]
    sem_count = [0]

    loads = []

    def load(src, dst):
        cp = pltpu.make_async_copy(src, dst, in_sem.at[len(loads)])
        cp.start()
        loads.append(cp)
        return cp

    lists = [load(slots_hbm, slots), load(counts_hbm, counts), load(edges_hbm, edges)]
    need_requests = load(requests_hbm, requests)
    need_w1 = [load(w1_hbm.at[q : q + 256], w1.at[q : q + 256]) for q in range(0, 1024, 256)]
    need_inputs = [load(inputs_hbm.at[q : q + 128], inputs.at[q : q + 128]) for q in (0, 128)]
    need_w2 = load(w2_hbm, w2)
    need_inputs += [load(inputs_hbm.at[q : q + 128], inputs.at[q : q + 128]) for q in (256, 384)]

    def device(xx, hh, cc, ll, yy):
        return (xx * 4 + hh * 2 + cc, ll * 4 + yy)

    def copy(src, dst, target):
        at = sem_count[0]
        sem_count[0] += 1
        return pltpu.make_async_remote_copy(
            src_ref=src, dst_ref=dst, send_sem=send_sem.at[at], recv_sem=recv_sem.at[at],
            device_id=target, device_id_type=MESH,
        )

    gone = []

    def left(cp):
        cp.wait_send()
        gone.append(id(cp))

    def xs(s):
        return (x + s) % NX

    def ys(s):
        return (y + s) % NY

    def ls(s):
        return (l + s) % NL

    barrier = pltpu.get_barrier_semaphore()
    plane = [(dx, dc) for dx in range(NX) for dc in range(NC) if dx or dc]
    ring = [(dl, dy) for dl in range(NL) for dy in range(NY) if dl or dy]
    peers = [device(xs(dx), h, (c + dc) % 2, l, y) for dx, dc in plane]
    peers += [device(x, h, c, ls(dl), ys(dy)) for dl, dy in ring]
    peers += [device(x, 1 - h, c, ls(dl), y) for dl in range(NL)]
    for peer in peers:
        pl.semaphore_signal(barrier, inc=1, device_id=peer, device_id_type=MESH)

    need_requests.wait()
    reqs[...] = jnp.zeros_like(reqs)
    for xx in range(NX):
        for cc in range(NC):
            for hh in range(NH):
                p = xx * 4 + hh * 2 + cc
                reqs[xx * 2 + cc, hh : hh + 1, :] = requests[p : p + 1, :]

    for cp in lists:
        cp.wait()
    live = lax.broadcasted_iota(jnp.int32, slots.shape, 0) < counts[...]
    place = ((slots[...] - x * 512) & 2047) ^ (h * 256 + c * 128)
    worth = jnp.where(live, edges[...], 0) << (((place >> 7) & 3) * 8)
    keys[...] = jnp.zeros_like(keys)
    keys[0:15, :] = (((place >> 9) << 7) | (place & 127)).astype(F32)
    keys[16:31, :] = worth.astype(F32)
    norms[...] = keys[...].T

    def weigh(at, _):
        r = pl.multiple_of(at * 16, 16)
        both = norms[pl.ds(r, 16), :].astype(jnp.int32)
        lane = lax.broadcasted_iota(jnp.int32, (16, 128), 1)
        total = [jnp.zeros((16, 128), jnp.int32) for _ in range(4)]
        for k in range(15):
            spot = jnp.broadcast_to(both[:, k : k + 1], (16, 128))
            value = jnp.broadcast_to(both[:, 16 + k : 17 + k], (16, 128))
            for part in range(4):
                total[part] = total[part] + jnp.where(spot == lane + part * 128, value, 0)
        for part in range(4):
            weights[part, pl.ds(r, 16), :] = total[part]
        return 0

    lax.fori_loop(0, 8, weigh, 0)

    for cp in need_w1:
        cp.wait()

    def forward(half):
        for q in (2 * half, 2 * half + 1):
            need_inputs[q].wait()
            for at in range(0, 1024, 256):
                pre = nn(inputs[q * 128 : q * 128 + 128, :], w1[:, at : at + 256])
                hidden[q * 128 : q * 128 + 128, at : at + 256] = jnp.maximum(pre, 0.0).astype(BF16)
        if half == 0:
            need_w2.wait()
        some = slice(half * 256, half * 256 + 256)
        codes[some, :] = nn(hidden[some, :], w2[...])
        sent[some, :] = codes[some, :].astype(BF16)
        sent_part[some, :] = sent[some, :] * (2.0 / 256.0)

    forward(0)
    pl.semaphore_wait(barrier, len(peers))

    ask = []
    for dx, dc in plane:
        j = dx * 2 + dc
        cp = copy(reqs.at[xs(dx) * 2 + (c + dc) % 2], asked.at[j], device(xs(dx), h, (c + dc) % 2, l, y))
        cp.start()
        ask.append(cp)
    to_next = [
        copy(sent.at[at : at + 256], far.at[3, at : at + 256], device(x, h, c, ls(1), y)) for at in (0, 256)
    ]
    to_next[0].start()
    forward(1)
    to_next[1].start()
    to_mate = []
    for e in range(2):
        cols = slice(e * 128, e * 128 + 128)
        to_mate.append(copy(sent.at[:, cols], mate.at[:, cols], device(x, 1 - h, c, l, y)))
    to_y = []
    for s in (1, 2, 3):
        cp = copy(sent, far.at[s - 1], device(x, h, c, l, ys(s)))
        to_y.append(cp)
        pl.when(y + s < NY)(cp.start)

    for g in range(8):
        xt[g * 128 : g * 128 + 128, :] = inputs[:, g * 128 : g * 128 + 128].T
    for cp in ask:
        cp.wait_recv()
    asked[0] = reqs[x * 2 + c]
    for j in range(8):
        norms2 = asked[j]
        asks_f[j * 8 : j * 8 + 8, :] = norms2.astype(F32)
    wishes[...] = asks_f[...].T

    lane = lax.broadcasted_iota(jnp.int32, (128, rows), 1).astype(F32)
    reply = {}

    def deliver(block, b, j, e):
        cols = slice(0, 256) if e is None else slice(e * 128, e * 128 + 128)
        got = nn(picks[b, j], block[:, cols]).astype(BF16)
        dx, dc = j // 2, j % 2
        spot = slice(b * 256 + dc * 128, b * 256 + dc * 128 + 128)
        if j == 0:
            table[0, spot, cols] = got
        else:
            found[b, j - 1, :, cols] = got
            cp = copy(
                found.at[b, j - 1, :, cols], table.at[dx, spot, cols],
                device(xs(NX - dx), h, (c + dc) % 2, l, y),
            )
            cp.start()
            reply.setdefault((b, dx), []).append(cp)

    turns = (2, 6, 4, 3, 7, 5, 1, 0)
    def choose(b):
        for j in turns:
            which = jnp.where((h + b) % 2 == 0, wishes[:, j * 8 : j * 8 + 1], wishes[:, j * 8 + 1 : j * 8 + 2])
            picks[b, j] = jnp.where(jnp.broadcast_to(which, (128, rows)) == lane, 1.0, 0.0).astype(BF16)
            if b == 0:
                deliver(sent, 0, j, None)

    choose(0)
    for cp in to_next:
        left(cp)
    to_mate[0].start()
    for cp in to_next:
        cp.wait_recv()
    for s in (1, 2, 3):
        cp = pltpu.make_async_remote_copy(
            src_ref=far.at[3], dst_ref=far.at[s - 1], send_sem=send_sem.at[11 + s - 1],
            recv_sem=recv_sem.at[11 + s - 1], device_id=device(x, h, c, l, ys(s)), device_id_type=MESH,
        )
        pl.when(y + s >= NY)(cp.start)
    lax.fori_loop(8, rows // 16, weigh, 0)
    left(to_mate[0])
    to_mate[1].start()
    choose(1)
    for g in range(8):
        ht[g * 128 : g * 128 + 128, :] = hidden[:, g * 128 : g * 128 + 128].T

    inv = 1.0 / 256.0
    own = sent[...].astype(F32)
    norm = jnp.sum(own * own, axis=1, keepdims=True)
    norms[...] = jnp.broadcast_to(norm * inv + 1.0, norms.shape)
    sums[...] = jnp.zeros_like(sums)
    acc[...] = jnp.zeros_like(acc)
    ones = jnp.ones((8, 256), BF16)

    def squares(block):
        z = block.astype(F32)
        z = z * z
        hi = z.astype(BF16)
        lo = (z - hi.astype(F32)).astype(BF16)
        return (nt(ones, hi) + nt(ones, lo))[0:1, :] * inv

    def pull(block, dx, b, offset):
        wide = block.shape[0]
        dist[:, 0:wide] = nt(sent_part[...], block[...])
        size = squares(block[...])

        def tile(at, _):
            r = pl.multiple_of(at * 64, 64)
            mine = norms[pl.ds(r, 64), :]
            total = sums[pl.ds(r, 64), :]
            for q in range(wide // 128):
                cols = slice(q * 128, q * 128 + 128)
                d = jnp.maximum((mine + size[:, cols]) - dist[pl.ds(r, 64), cols], 1.0)
                if dx is not None:
                    count = (weights[dx, pl.ds(r, 64), :] >> (8 * (b * 2 + q))) & 255
                    k = count.astype(F32) * (1.0 / d)
                else:
                    i = lax.broadcasted_iota(jnp.int32, (64, 128), 0)
                    j = lax.broadcasted_iota(jnp.int32, (64, 128), 1)
                    band = ((j - i) + (q * 128 - r - offset)) & (rows - 1)
                    k = jnp.where(band < NEGW, -1.0 / (d * (1.1 * (d - 1.0) + 0.1)), 0.0)
                k = k.astype(BF16)
                coef[pl.ds(r, 64), cols] = k
                total = total + k.astype(F32)
            sums[pl.ds(r, 64), :] = total
            return 0

        lax.fori_loop(0, rows // 64, tile, 0)
        acc[...] += nn(coef[:, 0:wide], block[...])

    def attract(b):
        for dx in (0, 1, 3, 2):
            for cp in reply[b, dx]:
                cp.wait_recv()
            pull(table.at[dx, b * 256 : b * 256 + 256], dx, b, None)

    def serve_mate(e):
        to_mate[e].wait_recv()
        for j in turns:
            deliver(mate, 1, j, e)

    attract(0)
    serve_mate(0)
    pull(far.at[3], None, None, offsets[3])
    serve_mate(1)
    for s in (1, 3, 2):
        to_y[s - 1].wait_recv()
        pull(far.at[s - 1], None, None, offsets[s - 1])
    attract(1)

    total = jnp.sum(sums[...], axis=1, keepdims=True)
    dcodes[...] = (scale * (total * codes[...] - acc[...])).astype(BF16)

    core = device(x, h, 1 - c, l, y)

    def backward(g, first, width):
        for at in range(first, first + width, 128):
            back = nt(dcodes[...], w2[at : at + 128, :])
            dpre[:, at : at + 128] = jnp.where(hidden[:, at : at + 128] > 0, back, 0.0).astype(BF16)
        g[...] = nn(xt[...], dpre[:, first : first + width])

    def part_rows(xx, hh, cc, yy):
        return pl.ds(pl.multiple_of(xx * 256 + hh * 128 + cc * 64 + yy * 16, 16), 16)

    each = [(xx, hh, yy) for xx in range(NX) for hh in range(NH) for yy in range(NY)]
    sends = []

    def go(src, dst, target):
        cp = copy(src, dst, target)
        cp.start()
        sends.append(cp)
        return cp

    def spot(kind, xx, hh, yy):
        return (xx, hh, yy) if kind == "a" else (yy, hh, xx)

    class Chunk:
        def __init__(self, kind, g, c_out, c_in, p_out, p_in, f, q_out, q_in):
            self.kind, self.g, self.c_out, self.c_in, self.p_out, self.p_in = kind, g, c_out, c_in, p_out, p_in
            self.f, self.q_out, self.q_in = f, q_out, q_in

        def near(self, s):
            return (xs(s), device(xs(s), h, c, l, y)) if self.kind == "a" else (ys(s), device(x, h, c, l, ys(s)))

        def beyond(self, s):
            return (ys(s), device(x, h, c, l, ys(s))) if self.kind == "a" else (xs(s), device(xs(s), h, c, l, y))

        def to_core(self):
            for xx, hh, yy in each:
                self.c_out[spot(self.kind, xx, hh, yy)] = self.g[part_rows(xx, hh, 1 - c, yy), :].astype(BF16)
            self.core = go(self.c_out, self.c_in, core)

        def first(self):
            self.core.wait_recv()
            for xx, hh, yy in each:
                at = spot(self.kind, xx, hh, yy)
                self.p_out[at] = (self.g[part_rows(xx, hh, c, yy), :] + self.c_in[at].astype(F32)).astype(BF16)
            self.one = []
            for s in (2, 1, 3):
                at, target = self.near(s)
                self.one.append(go(self.p_out.at[at], self.p_in.at[s - 1], target))
            mine = x if self.kind == "a" else y
            for far_at in range(4):
                for hh in range(NH):
                    rows_at = part_rows(x, hh, c, far_at) if self.kind == "a" else part_rows(far_at, hh, c, y)
                    self.f[hh, far_at] = self.g[rows_at, :] + self.c_in[mine, hh, far_at].astype(F32)

        def second(self):
            for cp in self.one:
                cp.wait_recv()
            for hh in range(NH):
                for far_at in range(4):
                    got = [self.p_in[s, hh, far_at].astype(F32) for s in range(3)]
                    self.f[hh, far_at] += got[0] + got[1] + got[2]
                    self.q_out[far_at, hh] = self.f[hh, far_at].astype(BF16)
            self.two = []
            for s in (2, 1, 3):
                at, target = self.beyond(s)
                self.two.append(go(self.q_out.at[at], self.q_in.at[s - 1], target))

        def result(self, hh):
            mine = y if self.kind == "a" else x
            got = [self.q_in[s, hh].astype(F32) for s in range(3)]
            return self.f[hh, mine] + got[0] + got[1] + got[2]

    class Pair:
        def __init__(self, a, b, zs_out, zs_in, whole):
            self.a, self.b, self.zs_out, self.zs_in, self.whole = a, b, zs_out, zs_in, whole

        def over_z(self):
            for cp in self.a.two + self.b.two:
                cp.wait_recv()
            for hh in range(NH):
                for half, chunk in enumerate((self.a, self.b)):
                    total = chunk.result(hh)
                    self.zs_out[hh, half] = total[0:8, :]
                    self.zs_out[hh, 2 + half] = total[8:16, :]
            self.zs = []
            for dh, dl in ((1, 0), (1, 2), (1, 1), (1, 3), (0, 2), (0, 1), (0, 3)):
                hh = (h + dh) % 2
                self.zs.append(
                    go(self.zs_out.at[hh, ls(dl)], self.zs_in.at[dh * 4 + dl], device(x, hh, c, ls(dl), y))
                )

        def spread(self):
            total = self.zs_out[h, l]
            for cp in self.zs:
                cp.wait_recv()
            for k in range(1, 8):
                total = total + self.zs_in[k]
            self.whole[y, l] = total
            self.along = {}
            self.last = []
            for dl in (2, 1, 3):
                piece = self.whole.at[y, l]
                self.along[dl] = go(piece, piece, device(x, h, c, ls(dl), y))
            self.pass_on(l)

        def pass_on(self, ll):
            for s in (2, 1, 3):
                piece = self.whole.at[y, ll]
                self.last.append(go(piece, piece, device(x, h, c, l, ys(s))))

        def relay(self):
            for dl in (1, 3, 2):
                self.along[dl].wait_recv()
                self.pass_on(ls(NL - dl))

    a0, b0 = Chunk("a", *pair0[0:8]), Chunk("b", *pair0[8:16])
    a1, b1 = Chunk("a", *pair1[0:8]), Chunk("b", *pair1[8:16])
    p0, p1 = Pair(a0, b0, *pair0[16:19]), Pair(a1, b1, *pair1[16:19])
    backward(b0.g, 0, 384)
    b0.to_core()
    backward(a0.g, 384, 384)
    a0.to_core()
    b0.first()
    a0.first()
    a1.g[...] = nn(ht[...], dcodes[...])
    a1.to_core()
    backward(b1.g, 768, 256)
    b1.to_core()
    for cp in a0.one + b0.one:
        left(cp)
    a1.first()
    b1.first()
    b0.second()
    a0.second()
    a1.second()
    b1.second()
    p0.over_z()
    p1.over_z()
    p0.spread()
    p1.spread()
    p0.relay()
    p1.relay()
    for cp in p0.last:
        cp.wait_recv()
    out0[...] = p0.whole[...]
    for cp in p1.last:
        cp.wait_recv()
    out1[...] = p1.whole[...]

    for cp in ask + to_next + to_mate + to_y + sum(reply.values(), []) + sends:
        if id(cp) not in gone:
            cp.wait_send()


def pair_scratch(width):
    chunk = [
        pltpu.VMEM((1024, width), F32),
        pltpu.VMEM((4, 2, 4, 16, width), BF16),
        pltpu.VMEM((4, 2, 4, 16, width), BF16),
        pltpu.VMEM((4, 2, 4, 16, width), BF16),
        pltpu.VMEM((3, 2, 4, 16, width), BF16),
        pltpu.VMEM((2, 4, 16, width), F32),
        pltpu.VMEM((4, 2, 16, width), BF16),
        pltpu.VMEM((3, 2, 16, width), BF16),
    ]
    shared = [
        pltpu.VMEM((2, 4, 8, width), F32),
        pltpu.VMEM((8, 8, width), F32),
        pltpu.VMEM((4, 4, 8, width), F32),
    ]
    return chunk + chunk + shared


def assemble(whole0, whole1, out_first, out_second):
    for yy in range(NY):
        for ll in range(NL):
            at = slice(yy * 16 + (ll // 2) * 8, yy * 16 + (ll // 2) * 8 + 8)
            if ll % 2 == 0:
                out_first[at, 384:768] = whole0[yy, ll]
                out_second[at, :] = whole1[yy, ll]
            else:
                out_first[at, 0:384] = whole0[yy, ll]
                out_first[at, 768:1024] = whole1[yy, ll]


def shards(inputs, w_first, w_second, requests, slots, counts, edge_weight, offsets):
    rows = inputs.shape[0]
    total_rows = rows * lax.axis_size("wide") * lax.axis_size("narrow")
    scale = 2.0 / (slots.shape[1] * math.sqrt(total_rows))
    vmem = pl.BlockSpec(memory_space=pltpu.VMEM)
    smem = pl.BlockSpec(memory_space=pltpu.SMEM)
    anyplace = pl.BlockSpec(memory_space=pl.ANY)
    whole0, whole1 = pl.pallas_call(
        lambda *refs: step(scale, *refs),
        out_shape=(
            jax.ShapeDtypeStruct((NY, NL, 8, 384), F32),
            jax.ShapeDtypeStruct((NY, NL, 8, 256), F32),
        ),
        in_specs=[anyplace] * 7 + [smem],
        out_specs=(vmem, vmem),
        scratch_shapes=[
            pltpu.VMEM((512, 1024), BF16),
            pltpu.VMEM((1024, 1024), BF16),
            pltpu.VMEM((1024, 256), BF16),
            pltpu.VMEM((16, 128), jnp.int32),
            pltpu.VMEM((15, 512), jnp.int32),
            pltpu.VMEM((1, 512), jnp.int32),
            pltpu.VMEM((15, 512), jnp.int32),
            pltpu.SemaphoreType.DMA((16,)),
            pltpu.VMEM((2, 8, 128, 512), BF16),
            pltpu.VMEM((512, 256), BF16),
            pltpu.VMEM((512, 1024), BF16),
            pltpu.VMEM((512, 256), F32),
            pltpu.VMEM((512, 256), BF16),
            pltpu.VMEM((512, 256), BF16),
            pltpu.VMEM((4, 512, 256), BF16),
            pltpu.VMEM((8, 8, 128), jnp.int32),
            pltpu.VMEM((8, 8, 128), jnp.int32),
            pltpu.VMEM((128, 512), F32),
            pltpu.VMEM((2, 7, 128, 256), BF16),
            pltpu.VMEM((4, 512, 256), BF16),
            pltpu.VMEM((4, 512, 128), jnp.int32),
            pltpu.VMEM((512, 128), F32),
            pltpu.VMEM((1024, 512), BF16),
            pltpu.VMEM((1024, 512), BF16),
            pltpu.VMEM((512, 128), F32),
            pltpu.VMEM((512, 256), F32),
            pltpu.VMEM((512, 512), F32),
            pltpu.VMEM((512, 512), BF16),
            pltpu.VMEM((512, 1024), BF16),
            pltpu.VMEM((512, 256), BF16),
            pltpu.VMEM((128, 128), F32),
            pltpu.VMEM((128, 128), F32),
            pltpu.SemaphoreType.DMA((128,)),
            pltpu.SemaphoreType.DMA((128,)),
        ]
        + pair_scratch(384)
        + pair_scratch(256),
        compiler_params=pltpu.CompilerParams(
            collective_id=0, has_side_effects=True, vmem_limit_bytes=56 << 20
        ),
        cost_estimate=pl.CostEstimate(flops=9_000_000_000, bytes_accessed=5_000_000, transcendentals=0),
        name="embedding_step",
    )(
        inputs, w_first, w_second, requests, slots.T, counts.reshape(1, -1), edge_weight.T, offsets
    )
    return pl.pallas_call(
        assemble,
        out_shape=(jax.ShapeDtypeStruct((64, 1024), F32), jax.ShapeDtypeStruct((64, 256), F32)),
        in_specs=[vmem, vmem],
        out_specs=(vmem, vmem),
        name="assemble",
    )(whole0, whole1)


def solution(mesh):
    return jax.shard_map(
        shards,
        mesh=mesh,
        in_specs=(
            P(("wide", "narrow"), None),
            P(),
            P(),
            P(("wide", "narrow"), None),
            P(("wide", "narrow"), None),
            P(("wide", "narrow")),
            P(("wide", "narrow"), None),
            P(),
        ),
        out_specs=(P("wide", None), P("wide", None)),
        check_vma=False,
    )
```

```python
import math

import jax
import jax.numpy as jnp
from jax import lax
from jax.experimental import pallas as pl
from jax.experimental.pallas import tpu as pltpu
from jax.sharding import PartitionSpec as P

MESH = pl.DeviceIdType.MESH
F32 = jnp.float32
BF16 = jnp.bfloat16
NEGW = 8
NX, NH, NC, NL, NY = 4, 2, 2, 4, 4


def nt(a, b):
    return lax.dot_general(a, b, (((1,), (1,)), ((), ())), preferred_element_type=F32)


def nn(a, b):
    return jnp.dot(a, b, preferred_element_type=F32)


def step(
    scale, inputs_hbm, w1_hbm, w2_hbm, requests_hbm, slots_hbm, counts_hbm, edges_hbm, offsets, out0, out1,
    inputs, w1, w2, requests, slots, counts, edges, in_sem, picks, sent_part, hidden, codes, sent, mate, far, reqs, asked, keys, found, table, weights, norms,
    xt, ht, sums, acc, dist, coef, dpre, dcodes, asks_f, wishes, send_sem, recv_sem, *pairs,
):
    pair0, pair1 = pairs[:20], pairs[20:]
    w = lax.axis_index("wide")
    n = lax.axis_index("narrow")
    x, h, c = w // 4, (w // 2) % 2, w % 2
    l, y = n // 4, n % 4
    rows = inputs.shape[0]
    sem_count = [0]

    loads = []

    def load(src, dst):
        cp = pltpu.make_async_copy(src, dst, in_sem.at[len(loads)])
        cp.start()
        loads.append(cp)
        return cp

    lists = [load(slots_hbm, slots), load(counts_hbm, counts), load(edges_hbm, edges)]
    need_requests = load(requests_hbm, requests)
    need_w1 = [load(w1_hbm.at[q : q + 256], w1.at[q : q + 256]) for q in range(0, 1024, 256)]
    need_inputs = [load(inputs_hbm.at[q : q + 128], inputs.at[q : q + 128]) for q in (0, 128)]
    need_w2 = load(w2_hbm, w2)
    need_inputs += [load(inputs_hbm.at[q : q + 128], inputs.at[q : q + 128]) for q in (256, 384)]

    def device(xx, hh, cc, ll, yy):
        return (xx * 4 + hh * 2 + cc, ll * 4 + yy)

    def copy(src, dst, target):
        at = sem_count[0]
        sem_count[0] += 1
        return pltpu.make_async_remote_copy(
            src_ref=src, dst_ref=dst, send_sem=send_sem.at[at], recv_sem=recv_sem.at[at],
            device_id=target, device_id_type=MESH,
        )

    gone = []

    def left(cp):
        cp.wait_send()
        gone.append(id(cp))

    def xs(s):
        return (x + s) % NX

    def ys(s):
        return (y + s) % NY

    def ls(s):
        return (l + s) % NL

    barrier = pltpu.get_barrier_semaphore()
    plane = [(dx, dc) for dx in range(NX) for dc in range(NC) if dx or dc]
    ring = [(dl, dy) for dl in range(NL) for dy in range(NY) if dl or dy]
    peers = [device(xs(dx), h, (c + dc) % 2, l, y) for dx, dc in plane]
    peers += [device(x, h, c, ls(dl), ys(dy)) for dl, dy in ring]
    peers += [device(x, 1 - h, c, ls(dl), y) for dl in range(NL)]
    for peer in peers:
        pl.semaphore_signal(barrier, inc=1, device_id=peer, device_id_type=MESH)

    need_requests.wait()
    reqs[...] = jnp.zeros_like(reqs)
    for xx in range(NX):
        for cc in range(NC):
            for hh in range(NH):
                p = xx * 4 + hh * 2 + cc
                reqs[xx * 2 + cc, hh : hh + 1, :] = requests[p : p + 1, :]

    for cp in lists:
        cp.wait()
    live = lax.broadcasted_iota(jnp.int32, slots.shape, 0) < counts[...]
    place = ((slots[...] - x * 512) & 2047) ^ (h * 256 + c * 128)
    worth = jnp.where(live, edges[...], 0) << (((place >> 7) & 3) * 8)
    keys[...] = jnp.zeros_like(keys)
    keys[0:15, :] = (((place >> 9) << 7) | (place & 127)).astype(F32)
    keys[16:31, :] = worth.astype(F32)
    norms[...] = keys[...].T

    def weigh(at, _):
        r = pl.multiple_of(at * 16, 16)
        both = norms[pl.ds(r, 16), :].astype(jnp.int32)
        lane = lax.broadcasted_iota(jnp.int32, (16, 128), 1)
        total = [jnp.zeros((16, 128), jnp.int32) for _ in range(4)]
        for k in range(15):
            spot = jnp.broadcast_to(both[:, k : k + 1], (16, 128))
            value = jnp.broadcast_to(both[:, 16 + k : 17 + k], (16, 128))
            for part in range(4):
                total[part] = total[part] + jnp.where(spot == lane + part * 128, value, 0)
        for part in range(4):
            weights[part, pl.ds(r, 16), :] = total[part]
        return 0

    lax.fori_loop(0, 8, weigh, 0)

    for cp in need_w1:
        cp.wait()

    def forward(half):
        for q in (2 * half, 2 * half + 1):
            need_inputs[q].wait()
            for at in range(0, 1024, 256):
                pre = nn(inputs[q * 128 : q * 128 + 128, :], w1[:, at : at + 256])
                hidden[q * 128 : q * 128 + 128, at : at + 256] = jnp.maximum(pre, 0.0).astype(BF16)
        if half == 0:
            need_w2.wait()
        some = slice(half * 256, half * 256 + 256)
        codes[some, :] = nn(hidden[some, :], w2[...])
        sent[some, :] = codes[some, :].astype(BF16)
        sent_part[some, :] = sent[some, :] * (2.0 / 256.0)

    forward(0)
    pl.semaphore_wait(barrier, len(peers))

    ask = []
    for dx, dc in plane:
        j = dx * 2 + dc
        cp = copy(reqs.at[xs(dx) * 2 + (c + dc) % 2], asked.at[j], device(xs(dx), h, (c + dc) % 2, l, y))
        cp.start()
        ask.append(cp)
    to_next = [
        copy(sent.at[at : at + 256], far.at[3, at : at + 256], device(x, h, c, ls(1), y)) for at in (0, 256)
    ]
    to_next[0].start()
    forward(1)
    to_next[1].start()
    to_mate = []
    for e in range(2):
        cols = slice(e * 128, e * 128 + 128)
        to_mate.append(copy(sent.at[:, cols], mate.at[:, cols], device(x, 1 - h, c, l, y)))
    to_mate[0].start()
    to_y = []
    for s in (1, 2, 3):
        cp = copy(sent, far.at[s - 1], device(x, h, c, l, ys(s)))
        to_y.append(cp)
        pl.when(y + s < NY)(cp.start)

    for g in range(8):
        xt[g * 128 : g * 128 + 128, :] = inputs[:, g * 128 : g * 128 + 128].T
    for cp in ask:
        cp.wait_recv()
    asked[0] = reqs[x * 2 + c]
    for j in range(8):
        norms2 = asked[j]
        asks_f[j * 8 : j * 8 + 8, :] = norms2.astype(F32)
    wishes[...] = asks_f[...].T

    lane = lax.broadcasted_iota(jnp.int32, (128, rows), 1).astype(F32)
    reply = {}

    def deliver(block, b, j, e):
        cols = slice(0, 256) if e is None else slice(e * 128, e * 128 + 128)
        got = nn(picks[b, j], block[:, cols]).astype(BF16)
        dx, dc = j // 2, j % 2
        spot = slice(b * 256 + dc * 128, b * 256 + dc * 128 + 128)
        if j == 0:
            table[0, spot, cols] = got
        else:
            found[b, j - 1, :, cols] = got
            cp = copy(
                found.at[b, j - 1, :, cols], table.at[dx, spot, cols],
                device(xs(NX - dx), h, (c + dc) % 2, l, y),
            )
            cp.start()
            reply.setdefault((b, dx), []).append(cp)

    turns = (2, 6, 4, 3, 7, 5, 1, 0)
    def choose(b):
        for j in turns:
            which = jnp.where((h + b) % 2 == 0, wishes[:, j * 8 : j * 8 + 1], wishes[:, j * 8 + 1 : j * 8 + 2])
            picks[b, j] = jnp.where(jnp.broadcast_to(which, (128, rows)) == lane, 1.0, 0.0).astype(BF16)
            if b == 0:
                deliver(sent, 0, j, None)

    choose(0)
    for cp in to_next:
        left(cp)
    to_mate[1].start()
    for cp in to_next:
        cp.wait_recv()
    for s in (1, 2, 3):
        cp = pltpu.make_async_remote_copy(
            src_ref=far.at[3], dst_ref=far.at[s - 1], send_sem=send_sem.at[11 + s - 1],
            recv_sem=recv_sem.at[11 + s - 1], device_id=device(x, h, c, l, ys(s)), device_id_type=MESH,
        )
        pl.when(y + s >= NY)(cp.start)
    lax.fori_loop(8, rows // 16, weigh, 0)
    choose(1)
    for g in range(8):
        ht[g * 128 : g * 128 + 128, :] = hidden[:, g * 128 : g * 128 + 128].T

    inv = 1.0 / 256.0
    own = sent[...].astype(F32)
    norm = jnp.sum(own * own, axis=1, keepdims=True)
    norms[...] = jnp.broadcast_to(norm * inv + 1.0, norms.shape)
    sums[...] = jnp.zeros_like(sums)
    acc[...] = jnp.zeros_like(acc)
    ones = jnp.ones((8, 256), BF16)

    def squares(block):
        z = block.astype(F32)
        z = z * z
        hi = z.astype(BF16)
        lo = (z - hi.astype(F32)).astype(BF16)
        return (nt(ones, hi) + nt(ones, lo))[0:1, :] * inv

    def pull(block, dx, b, offset):
        wide = block.shape[0]
        dist[:, 0:wide] = nt(sent_part[...], block[...])
        size = squares(block[...])

        def tile(at, _):
            r = pl.multiple_of(at * 64, 64)
            mine = norms[pl.ds(r, 64), :]
            total = sums[pl.ds(r, 64), :]
            for q in range(wide // 128):
                cols = slice(q * 128, q * 128 + 128)
                d = jnp.maximum((mine + size[:, cols]) - dist[pl.ds(r, 64), cols], 1.0)
                if dx is not None:
                    count = (weights[dx, pl.ds(r, 64), :] >> (8 * (b * 2 + q))) & 255
                    k = count.astype(F32) * (1.0 / d)
                else:
                    i = lax.broadcasted_iota(jnp.int32, (64, 128), 0)
                    j = lax.broadcasted_iota(jnp.int32, (64, 128), 1)
                    band = ((j - i) + (q * 128 - r - offset)) & (rows - 1)
                    k = jnp.where(band < NEGW, -1.0 / (d * (1.1 * (d - 1.0) + 0.1)), 0.0)
                k = k.astype(BF16)
                coef[pl.ds(r, 64), cols] = k
                total = total + k.astype(F32)
            sums[pl.ds(r, 64), :] = total
            return 0

        lax.fori_loop(0, rows // 64, tile, 0)
        acc[...] += nn(coef[:, 0:wide], block[...])

    def attract(b):
        for dx in (0, 1, 3, 2):
            for cp in reply[b, dx]:
                cp.wait_recv()
            pull(table.at[dx, b * 256 : b * 256 + 256], dx, b, None)

    def serve_mate(e):
        to_mate[e].wait_recv()
        for j in turns:
            deliver(mate, 1, j, e)

    attract(0)
    serve_mate(0)
    pull(far.at[3], None, None, offsets[3])
    serve_mate(1)
    for s in (1, 3, 2):
        to_y[s - 1].wait_recv()
        pull(far.at[s - 1], None, None, offsets[s - 1])
    attract(1)

    total = jnp.sum(sums[...], axis=1, keepdims=True)
    dcodes[...] = (scale * (total * codes[...] - acc[...])).astype(BF16)

    core = device(x, h, 1 - c, l, y)

    def backward(g, first, width):
        for at in range(first, first + width, 128):
            back = nt(dcodes[...], w2[at : at + 128, :])
            dpre[:, at : at + 128] = jnp.where(hidden[:, at : at + 128] > 0, back, 0.0).astype(BF16)
        g[...] = nn(xt[...], dpre[:, first : first + width])

    def part_rows(xx, hh, cc, yy):
        return pl.ds(pl.multiple_of(xx * 256 + hh * 128 + cc * 64 + yy * 16, 16), 16)

    each = [(xx, hh, yy) for xx in range(NX) for hh in range(NH) for yy in range(NY)]
    sends = []

    def go(src, dst, target):
        cp = copy(src, dst, target)
        cp.start()
        sends.append(cp)
        return cp

    def spot(kind, xx, hh, yy):
        return (xx, hh, yy) if kind == "a" else (yy, hh, xx)

    class Chunk:
        def __init__(self, kind, g, c_out, c_in, p_out, p_in, f, q_out, q_in):
            self.kind, self.g, self.c_out, self.c_in, self.p_out, self.p_in = kind, g, c_out, c_in, p_out, p_in
            self.f, self.q_out, self.q_in = f, q_out, q_in

        def near(self, s):
            return (xs(s), device(xs(s), h, c, l, y)) if self.kind == "a" else (ys(s), device(x, h, c, l, ys(s)))

        def beyond(self, s):
            return (ys(s), device(x, h, c, l, ys(s))) if self.kind == "a" else (xs(s), device(xs(s), h, c, l, y))

        def to_core(self):
            for xx, hh, yy in each:
                self.c_out[spot(self.kind, xx, hh, yy)] = self.g[part_rows(xx, hh, 1 - c, yy), :].astype(BF16)
            self.core = go(self.c_out, self.c_in, core)

        def first(self):
            self.core.wait_recv()
            for xx, hh, yy in each:
                at = spot(self.kind, xx, hh, yy)
                self.p_out[at] = (self.g[part_rows(xx, hh, c, yy), :] + self.c_in[at].astype(F32)).astype(BF16)
            self.one = []
            for s in (2, 1, 3):
                at, target = self.near(s)
                self.one.append(go(self.p_out.at[at], self.p_in.at[s - 1], target))
            mine = x if self.kind == "a" else y
            for far_at in range(4):
                for hh in range(NH):
                    rows_at = part_rows(x, hh, c, far_at) if self.kind == "a" else part_rows(far_at, hh, c, y)
                    self.f[hh, far_at] = self.g[rows_at, :] + self.c_in[mine, hh, far_at].astype(F32)

        def second(self):
            for cp in self.one:
                cp.wait_recv()
            for hh in range(NH):
                for far_at in range(4):
                    got = [self.p_in[s, hh, far_at].astype(F32) for s in range(3)]
                    self.f[hh, far_at] += got[0] + got[1] + got[2]
                    self.q_out[far_at, hh] = self.f[hh, far_at].astype(BF16)
            self.two = []
            for s in (2, 1, 3):
                at, target = self.beyond(s)
                self.two.append(go(self.q_out.at[at], self.q_in.at[s - 1], target))

        def result(self, hh):
            mine = y if self.kind == "a" else x
            got = [self.q_in[s, hh].astype(F32) for s in range(3)]
            return self.f[hh, mine] + got[0] + got[1] + got[2]

    class Pair:
        def __init__(self, a, b, by_columns, zs_own, zs_out, zs_in, whole):
            self.a, self.b, self.by_columns, self.zs_own = a, b, by_columns, zs_own
            self.zs_out, self.zs_in, self.whole = zs_out, zs_in, whole

        def over_z(self):
            for cp in self.a.two + self.b.two:
                cp.wait_recv()
            for hh in range(NH):
                for half, chunk in enumerate((self.a, self.b)):
                    total = chunk.result(hh)
                    if self.by_columns:
                        pieces = ((2 * half, total[:, 0:256]), (2 * half + 1, total[:, 256:512]))
                    else:
                        pieces = ((half, total[0:8, :]), (2 + half, total[8:16, :]))
                    for ll, piece in pieces:
                        self.zs_own[hh, ll] = piece
                        self.zs_out[hh, ll] = piece.astype(self.zs_out.dtype)
            self.zs = []
            for dh, dl in ((1, 0), (1, 2), (1, 1), (1, 3), (0, 2), (0, 1), (0, 3)):
                hh = (h + dh) % 2
                self.zs.append(
                    go(self.zs_out.at[hh, ls(dl)], self.zs_in.at[dh * 4 + dl], device(x, hh, c, ls(dl), y))
                )

        def spread(self):
            total = self.zs_own[h, l]
            for cp in self.zs:
                cp.wait_recv()
            for k in range(1, 8):
                total = total + self.zs_in[k].astype(F32)
            self.whole[y, l] = total
            self.along = {}
            self.last = []
            for dl in (2, 1, 3):
                piece = self.whole.at[y, l]
                self.along[dl] = go(piece, piece, device(x, h, c, ls(dl), y))
            self.pass_on(l)

        def pass_on(self, ll):
            for s in (2, 1, 3):
                piece = self.whole.at[y, ll]
                self.last.append(go(piece, piece, device(x, h, c, l, ys(s))))

        def relay(self):
            for dl in (1, 3, 2):
                self.along[dl].wait_recv()
                self.pass_on(ls(NL - dl))

    a0, b0 = Chunk("a", *pair0[0:8]), Chunk("b", *pair0[8:16])
    a1, b1 = Chunk("a", *pair1[0:8]), Chunk("b", *pair1[8:16])
    p0, p1 = Pair(a0, b0, True, *pair0[16:20]), Pair(a1, b1, False, *pair1[16:20])
    backward(b0.g, 0, 512)
    b0.to_core()
    backward(a0.g, 512, 512)
    a0.to_core()
    b0.first()
    a0.first()
    a1.g[...] = nn(ht[...], dcodes[:, 0:128])
    a1.to_core()
    b1.g[...] = nn(ht[...], dcodes[:, 128:256])
    b1.to_core()
    for cp in a0.one + b0.one:
        left(cp)
    a1.first()
    b1.first()
    b0.second()
    a0.second()
    a1.second()
    b1.second()
    p0.over_z()
    p1.over_z()
    p0.spread()
    p1.spread()
    p0.relay()
    p1.relay()
    for cp in p0.last:
        cp.wait_recv()
    out0[...] = p0.whole[...]
    for cp in p1.last:
        cp.wait_recv()
    out1[...] = p1.whole[...]

    for cp in ask + to_next + to_mate + to_y + sum(reply.values(), []) + sends:
        if id(cp) not in gone:
            cp.wait_send()


def pair_scratch(width, piece, over_z):
    chunk = [
        pltpu.VMEM((1024, width), F32),
        pltpu.VMEM((4, 2, 4, 16, width), BF16),
        pltpu.VMEM((4, 2, 4, 16, width), BF16),
        pltpu.VMEM((4, 2, 4, 16, width), BF16),
        pltpu.VMEM((3, 2, 4, 16, width), BF16),
        pltpu.VMEM((2, 4, 16, width), F32),
        pltpu.VMEM((4, 2, 16, width), BF16),
        pltpu.VMEM((3, 2, 16, width), BF16),
    ]
    shared = [
        pltpu.VMEM((2, 4, *piece), F32),
        pltpu.VMEM((2, 4, *piece), over_z),
        pltpu.VMEM((8, *piece), over_z),
        pltpu.VMEM((4, 4, *piece), F32),
    ]
    return chunk + chunk + shared


def assemble(whole0, whole1, out_first, out_second):
    for yy in range(NY):
        for ll in range(NL):
            first = (1 - ll // 2) * 512 + (ll % 2) * 256
            out_first[yy * 16 : yy * 16 + 16, first : first + 256] = whole0[yy, ll]
            at = yy * 16 + (ll // 2) * 8
            out_second[at : at + 8, (ll % 2) * 128 : (ll % 2) * 128 + 128] = whole1[yy, ll]


def shards(inputs, w_first, w_second, requests, slots, counts, edge_weight, offsets):
    rows = inputs.shape[0]
    total_rows = rows * lax.axis_size("wide") * lax.axis_size("narrow")
    scale = 2.0 / (slots.shape[1] * math.sqrt(total_rows))
    vmem = pl.BlockSpec(memory_space=pltpu.VMEM)
    smem = pl.BlockSpec(memory_space=pltpu.SMEM)
    anyplace = pl.BlockSpec(memory_space=pl.ANY)
    whole0, whole1 = pl.pallas_call(
        lambda *refs: step(scale, *refs),
        out_shape=(
            jax.ShapeDtypeStruct((NY, NL, 16, 256), F32),
            jax.ShapeDtypeStruct((NY, NL, 8, 128), F32),
        ),
        in_specs=[anyplace] * 7 + [smem],
        out_specs=(vmem, vmem),
        scratch_shapes=[
            pltpu.VMEM((512, 1024), BF16),
            pltpu.VMEM((1024, 1024), BF16),
            pltpu.VMEM((1024, 256), BF16),
            pltpu.VMEM((16, 128), jnp.int32),
            pltpu.VMEM((15, 512), jnp.int32),
            pltpu.VMEM((1, 512), jnp.int32),
            pltpu.VMEM((15, 512), jnp.int32),
            pltpu.SemaphoreType.DMA((16,)),
            pltpu.VMEM((2, 8, 128, 512), BF16),
            pltpu.VMEM((512, 256), BF16),
            pltpu.VMEM((512, 1024), BF16),
            pltpu.VMEM((512, 256), F32),
            pltpu.VMEM((512, 256), BF16),
            pltpu.VMEM((512, 256), BF16),
            pltpu.VMEM((4, 512, 256), BF16),
            pltpu.VMEM((8, 8, 128), jnp.int32),
            pltpu.VMEM((8, 8, 128), jnp.int32),
            pltpu.VMEM((128, 512), F32),
            pltpu.VMEM((2, 7, 128, 256), BF16),
            pltpu.VMEM((4, 512, 256), BF16),
            pltpu.VMEM((4, 512, 128), jnp.int32),
            pltpu.VMEM((512, 128), F32),
            pltpu.VMEM((1024, 512), BF16),
            pltpu.VMEM((1024, 512), BF16),
            pltpu.VMEM((512, 128), F32),
            pltpu.VMEM((512, 256), F32),
            pltpu.VMEM((512, 512), F32),
            pltpu.VMEM((512, 512), BF16),
            pltpu.VMEM((512, 1024), BF16),
            pltpu.VMEM((512, 256), BF16),
            pltpu.VMEM((128, 128), F32),
            pltpu.VMEM((128, 128), F32),
            pltpu.SemaphoreType.DMA((128,)),
            pltpu.SemaphoreType.DMA((128,)),
        ]
        + pair_scratch(512, (16, 256), BF16)
        + pair_scratch(128, (8, 128), F32),
        compiler_params=pltpu.CompilerParams(
            collective_id=0, has_side_effects=True, vmem_limit_bytes=56 << 20
        ),
        cost_estimate=pl.CostEstimate(flops=9_000_000_000, bytes_accessed=5_000_000, transcendentals=0),
        name="embedding_step",
    )(
        inputs, w_first, w_second, requests, slots.T, counts.reshape(1, -1), edge_weight.T, offsets
    )
    return pl.pallas_call(
        assemble,
        out_shape=(jax.ShapeDtypeStruct((64, 1024), F32), jax.ShapeDtypeStruct((64, 256), F32)),
        in_specs=[vmem, vmem],
        out_specs=(vmem, vmem),
        name="assemble",
    )(whole0, whole1)


def solution(mesh):
    return jax.shard_map(
        shards,
        mesh=mesh,
        in_specs=(
            P(("wide", "narrow"), None),
            P(),
            P(),
            P(("wide", "narrow"), None),
            P(("wide", "narrow"), None),
            P(("wide", "narrow")),
            P(("wide", "narrow"), None),
            P(),
        ),
        out_specs=(P("wide", None), P("wide", None)),
        check_vma=False,
    )
```

```python
import math

import jax
import jax.numpy as jnp
from jax import lax
from jax.experimental import pallas as pl
from jax.experimental.pallas import tpu as pltpu
from jax.sharding import PartitionSpec as P

MESH = pl.DeviceIdType.MESH
F32 = jnp.float32
BF16 = jnp.bfloat16
NEGW = 8
NX, NH, NC, NL, NY = 4, 2, 2, 4, 4


def nt(a, b):
    return lax.dot_general(a, b, (((1,), (1,)), ((), ())), preferred_element_type=F32)


def nn(a, b):
    return jnp.dot(a, b, preferred_element_type=F32)


def step(
    scale, inputs_hbm, w1_hbm, w2_hbm, requests_hbm, slots_hbm, counts_hbm, edges_hbm, offsets, out0, out1,
    inputs, w1, w2, requests, slots, counts, edges, in_sem, picks, sent_part, hidden, codes, sent, mate, far, reqs, asked, keys, found, table, weights, norms,
    xt, ht, sums, acc, dist, coef, dpre, dcodes, asks_f, wishes, send_sem, recv_sem, *pairs,
):
    pair0, pair1 = pairs[:20], pairs[20:]
    w = lax.axis_index("wide")
    n = lax.axis_index("narrow")
    x, h, c = w // 4, (w // 2) % 2, w % 2
    l, y = n // 4, n % 4
    rows = inputs.shape[0]
    sem_count = [0]

    loads = []

    def load(src, dst):
        cp = pltpu.make_async_copy(src, dst, in_sem.at[len(loads)])
        cp.start()
        loads.append(cp)
        return cp

    lists = [load(slots_hbm, slots), load(counts_hbm, counts), load(edges_hbm, edges)]
    need_requests = load(requests_hbm, requests)
    need_w1 = [load(w1_hbm.at[q : q + 256], w1.at[q : q + 256]) for q in range(0, 1024, 256)]
    need_inputs = [load(inputs_hbm.at[q : q + 128], inputs.at[q : q + 128]) for q in (0, 128)]
    need_w2 = load(w2_hbm, w2)
    need_inputs += [load(inputs_hbm.at[q : q + 128], inputs.at[q : q + 128]) for q in (256, 384)]

    def device(xx, hh, cc, ll, yy):
        return (xx * 4 + hh * 2 + cc, ll * 4 + yy)

    def copy(src, dst, target):
        at = sem_count[0]
        sem_count[0] += 1
        return pltpu.make_async_remote_copy(
            src_ref=src, dst_ref=dst, send_sem=send_sem.at[at], recv_sem=recv_sem.at[at],
            device_id=target, device_id_type=MESH,
        )

    gone = []

    def left(cp):
        cp.wait_send()
        gone.append(id(cp))

    def xs(s):
        return (x + s) % NX

    def ys(s):
        return (y + s) % NY

    def ls(s):
        return (l + s) % NL

    barrier = pltpu.get_barrier_semaphore()
    plane = [(dx, dc) for dx in range(NX) for dc in range(NC) if dx or dc]
    ring = [(dl, dy) for dl in range(NL) for dy in range(NY) if dl or dy]
    peers = [device(xs(dx), h, (c + dc) % 2, l, y) for dx, dc in plane]
    peers += [device(x, h, c, ls(dl), ys(dy)) for dl, dy in ring]
    peers += [device(x, 1 - h, c, ls(dl), y) for dl in range(NL)]
    for peer in peers:
        pl.semaphore_signal(barrier, inc=1, device_id=peer, device_id_type=MESH)

    need_requests.wait()
    reqs[...] = jnp.zeros_like(reqs)
    for xx in range(NX):
        for cc in range(NC):
            for hh in range(NH):
                p = xx * 4 + hh * 2 + cc
                reqs[xx * 2 + cc, hh : hh + 1, :] = requests[p : p + 1, :]

    for cp in lists:
        cp.wait()
    live = lax.broadcasted_iota(jnp.int32, slots.shape, 0) < counts[...]
    place = ((slots[...] - x * 512) & 2047) ^ (h * 256 + c * 128)
    worth = jnp.where(live, edges[...], 0) << (((place >> 7) & 3) * 8)
    keys[...] = jnp.zeros_like(keys)
    keys[0:15, :] = (((place >> 9) << 7) | (place & 127)).astype(F32)
    keys[16:31, :] = worth.astype(F32)
    norms[...] = keys[...].T

    def weigh(at, _):
        r = pl.multiple_of(at * 16, 16)
        both = norms[pl.ds(r, 16), :].astype(jnp.int32)
        lane = lax.broadcasted_iota(jnp.int32, (16, 128), 1)
        total = [jnp.zeros((16, 128), jnp.int32) for _ in range(4)]
        for k in range(15):
            spot = jnp.broadcast_to(both[:, k : k + 1], (16, 128))
            value = jnp.broadcast_to(both[:, 16 + k : 17 + k], (16, 128))
            for part in range(4):
                total[part] = total[part] + jnp.where(spot == lane + part * 128, value, 0)
        for part in range(4):
            weights[part, pl.ds(r, 16), :] = total[part]
        return 0


    for cp in need_w1:
        cp.wait()

    def forward(half):
        for q in (2 * half, 2 * half + 1):
            need_inputs[q].wait()
            for at in range(0, 1024, 256):
                pre = nn(inputs[q * 128 : q * 128 + 128, :], w1[:, at : at + 256])
                hidden[q * 128 : q * 128 + 128, at : at + 256] = jnp.maximum(pre, 0.0).astype(BF16)
        if half == 0:
            need_w2.wait()
        some = slice(half * 256, half * 256 + 256)
        codes[some, :] = nn(hidden[some, :], w2[...])
        sent[some, :] = codes[some, :].astype(BF16)
        sent_part[some, :] = sent[some, :] * (2.0 / 256.0)

    forward(0)
    pl.semaphore_wait(barrier, len(peers))

    ask = []
    for dx, dc in plane:
        j = dx * 2 + dc
        cp = copy(reqs.at[xs(dx) * 2 + (c + dc) % 2], asked.at[j], device(xs(dx), h, (c + dc) % 2, l, y))
        cp.start()
        ask.append(cp)
    to_next = [
        copy(sent.at[at : at + 256], far.at[3, at : at + 256], device(x, h, c, ls(1), y)) for at in (0, 256)
    ]
    to_next[0].start()
    forward(1)
    to_next[1].start()
    to_mate = []
    for e in range(2):
        cols = slice(e * 128, e * 128 + 128)
        to_mate.append(copy(sent.at[:, cols], mate.at[:, cols], device(x, 1 - h, c, l, y)))
    to_mate[0].start()
    to_y = []
    for s in (1, 2, 3):
        cp = copy(sent, far.at[s - 1], device(x, h, c, l, ys(s)))
        to_y.append(cp)
        pl.when(y + s < NY)(cp.start)

    for g in range(8):
        xt[g * 128 : g * 128 + 128, :] = inputs[:, g * 128 : g * 128 + 128].T
    for cp in ask:
        cp.wait_recv()
    asked[0] = reqs[x * 2 + c]
    for j in range(8):
        norms2 = asked[j]
        asks_f[j * 8 : j * 8 + 8, :] = norms2.astype(F32)
    wishes[...] = asks_f[...].T

    lane = lax.broadcasted_iota(jnp.int32, (128, rows), 1).astype(F32)
    reply = {}

    def deliver(block, b, e):
        cols = slice(0, 256) if e is None else slice(e * 128, e * 128 + 128)
        got = nn(picks[b].reshape(8 * 128, rows), block[:, cols]).astype(BF16)
        found[b, :, :, cols] = got.reshape(8, 128, got.shape[1])
        for j in turns:
            dx, dc = j // 2, j % 2
            spot = slice(b * 256 + dc * 128, b * 256 + dc * 128 + 128)
            if j == 0:
                table[0, spot, cols] = found[b, 0, :, cols]
            else:
                cp = copy(
                    found.at[b, j, :, cols], table.at[dx, spot, cols],
                    device(xs(NX - dx), h, (c + dc) % 2, l, y),
                )
                cp.start()
                reply.setdefault((b, dx), []).append(cp)

    turns = (4, 5, 2, 6, 3, 7, 1, 0)

    def choose(b):
        for j in turns:
            which = jnp.where((h + b) % 2 == 0, wishes[:, j * 8 : j * 8 + 1], wishes[:, j * 8 + 1 : j * 8 + 2])
            picks[b, j] = jnp.where(jnp.broadcast_to(which, (128, rows)) == lane, 1.0, 0.0).astype(BF16)

    choose(0)
    deliver(sent, 0, None)
    for cp in to_next:
        left(cp)
    to_mate[1].start()
    for cp in to_next:
        cp.wait_recv()
    for s in (1, 2, 3):
        cp = pltpu.make_async_remote_copy(
            src_ref=far.at[3], dst_ref=far.at[s - 1], send_sem=send_sem.at[11 + s - 1],
            recv_sem=recv_sem.at[11 + s - 1], device_id=device(x, h, c, l, ys(s)), device_id_type=MESH,
        )
        pl.when(y + s >= NY)(cp.start)
    lax.fori_loop(0, rows // 16, weigh, 0)
    choose(1)
    for g in range(8):
        ht[g * 128 : g * 128 + 128, :] = hidden[:, g * 128 : g * 128 + 128].T

    inv = 1.0 / 256.0
    own = sent[...].astype(F32)
    norm = jnp.sum(own * own, axis=1, keepdims=True)
    norms[...] = jnp.broadcast_to(norm * inv + 1.0, norms.shape)
    sums[...] = jnp.zeros_like(sums)
    acc[...] = jnp.zeros_like(acc)
    ones = jnp.ones((8, 256), BF16)

    def squares(block):
        z = block.astype(F32)
        z = z * z
        hi = z.astype(BF16)
        lo = (z - hi.astype(F32)).astype(BF16)
        return (nt(ones, hi) + nt(ones, lo))[0:1, :] * inv

    def pull(block, dx, b, offset):
        wide = block.shape[0]
        dist[:, 0:wide] = nt(sent_part[...], block[...])
        size = squares(block[...])

        def tile(at, _):
            r = pl.multiple_of(at * 64, 64)
            mine = norms[pl.ds(r, 64), :]
            total = sums[pl.ds(r, 64), :]
            for q in range(wide // 128):
                cols = slice(q * 128, q * 128 + 128)
                d = jnp.maximum((mine + size[:, cols]) - dist[pl.ds(r, 64), cols], 1.0)
                if dx is not None:
                    count = (weights[dx, pl.ds(r, 64), :] >> (8 * (b * 2 + q))) & 255
                    k = count.astype(F32) * (1.0 / d)
                else:
                    i = lax.broadcasted_iota(jnp.int32, (64, 128), 0)
                    j = lax.broadcasted_iota(jnp.int32, (64, 128), 1)
                    band = ((j - i) + (q * 128 - r - offset)) & (rows - 1)
                    k = jnp.where(band < NEGW, -1.0 / (d * (1.1 * (d - 1.0) + 0.1)), 0.0)
                k = k.astype(BF16)
                coef[pl.ds(r, 64), cols] = k
                total = total + k.astype(F32)
            sums[pl.ds(r, 64), :] = total
            return 0

        lax.fori_loop(0, rows // 64, tile, 0)
        acc[...] += nn(coef[:, 0:wide], block[...])

    def attract(b):
        for dx in (0, 1, 3, 2):
            for cp in reply[b, dx]:
                cp.wait_recv()
            pull(table.at[dx, b * 256 : b * 256 + 256], dx, b, None)

    def serve_mate(e):
        to_mate[e].wait_recv()
        deliver(mate, 1, e)

    attract(0)
    serve_mate(0)
    pull(far.at[3], None, None, offsets[3])
    serve_mate(1)
    for s in (1, 3, 2):
        to_y[s - 1].wait_recv()
        pull(far.at[s - 1], None, None, offsets[s - 1])
    attract(1)

    total = jnp.sum(sums[...], axis=1, keepdims=True)
    dcodes[...] = (scale * (total * codes[...] - acc[...])).astype(BF16)

    core = device(x, h, 1 - c, l, y)

    def backward(g, first, width):
        for at in range(first, first + width, 128):
            back = nt(dcodes[...], w2[at : at + 128, :])
            dpre[:, at : at + 128] = jnp.where(hidden[:, at : at + 128] > 0, back, 0.0).astype(BF16)
        g[...] = nn(xt[...], dpre[:, first : first + width])

    def part_rows(xx, hh, cc, yy):
        return pl.ds(pl.multiple_of(xx * 256 + hh * 128 + cc * 64 + yy * 16, 16), 16)

    each = [(xx, hh, yy) for xx in range(NX) for hh in range(NH) for yy in range(NY)]
    sends = []

    def go(src, dst, target):
        cp = copy(src, dst, target)
        cp.start()
        sends.append(cp)
        return cp

    def spot(kind, xx, hh, yy):
        return (xx, hh, yy) if kind == "a" else (yy, hh, xx)

    class Chunk:
        def __init__(self, kind, g, c_out, c_in, p_out, p_in, f, q_out, q_in):
            self.kind, self.g, self.c_out, self.c_in, self.p_out, self.p_in = kind, g, c_out, c_in, p_out, p_in
            self.f, self.q_out, self.q_in = f, q_out, q_in

        def near(self, s):
            return (xs(s), device(xs(s), h, c, l, y)) if self.kind == "a" else (ys(s), device(x, h, c, l, ys(s)))

        def beyond(self, s):
            return (ys(s), device(x, h, c, l, ys(s))) if self.kind == "a" else (xs(s), device(xs(s), h, c, l, y))

        def to_core(self):
            for xx, hh, yy in each:
                self.c_out[spot(self.kind, xx, hh, yy)] = self.g[part_rows(xx, hh, 1 - c, yy), :].astype(BF16)
            self.core = go(self.c_out, self.c_in, core)

        def first(self):
            self.core.wait_recv()
            for xx, hh, yy in each:
                at = spot(self.kind, xx, hh, yy)
                self.p_out[at] = (self.g[part_rows(xx, hh, c, yy), :] + self.c_in[at].astype(F32)).astype(BF16)
            self.one = []
            for s in (2, 1, 3):
                at, target = self.near(s)
                self.one.append(go(self.p_out.at[at], self.p_in.at[s - 1], target))
            mine = x if self.kind == "a" else y
            for far_at in range(4):
                for hh in range(NH):
                    rows_at = part_rows(x, hh, c, far_at) if self.kind == "a" else part_rows(far_at, hh, c, y)
                    self.f[hh, far_at] = self.g[rows_at, :] + self.c_in[mine, hh, far_at].astype(F32)

        def second(self):
            for cp in self.one:
                cp.wait_recv()
            for hh in range(NH):
                for far_at in range(4):
                    got = [self.p_in[s, hh, far_at].astype(F32) for s in range(3)]
                    self.f[hh, far_at] += got[0] + got[1] + got[2]
                    self.q_out[far_at, hh] = self.f[hh, far_at].astype(BF16)
            self.two = []
            for s in (2, 1, 3):
                at, target = self.beyond(s)
                self.two.append(go(self.q_out.at[at], self.q_in.at[s - 1], target))

        def result(self, hh):
            mine = y if self.kind == "a" else x
            got = [self.q_in[s, hh].astype(F32) for s in range(3)]
            return self.f[hh, mine] + got[0] + got[1] + got[2]

    class Pair:
        def __init__(self, a, b, by_columns, zs_own, zs_out, zs_in, whole):
            self.a, self.b, self.by_columns, self.zs_own = a, b, by_columns, zs_own
            self.zs_out, self.zs_in, self.whole = zs_out, zs_in, whole

        def over_z(self):
            for cp in self.a.two + self.b.two:
                cp.wait_recv()
            for hh in range(NH):
                for half, chunk in enumerate((self.a, self.b)):
                    total = chunk.result(hh)
                    if self.by_columns:
                        pieces = ((2 * half, total[:, 0:256]), (2 * half + 1, total[:, 256:512]))
                    else:
                        pieces = ((half, total[0:8, :]), (2 + half, total[8:16, :]))
                    for ll, piece in pieces:
                        self.zs_own[hh, ll] = piece
                        self.zs_out[hh, ll] = piece.astype(self.zs_out.dtype)
            self.zs = []
            for dh, dl in ((1, 0), (1, 2), (1, 1), (1, 3), (0, 2), (0, 1), (0, 3)):
                hh = (h + dh) % 2
                self.zs.append(
                    go(self.zs_out.at[hh, ls(dl)], self.zs_in.at[dh * 4 + dl], device(x, hh, c, ls(dl), y))
                )

        def spread(self):
            total = self.zs_own[h, l]
            for cp in self.zs:
                cp.wait_recv()
            for k in range(1, 8):
                total = total + self.zs_in[k].astype(F32)
            self.whole[y, l] = total
            self.along = {}
            self.last = []
            for dl in (2, 1, 3):
                piece = self.whole.at[y, l]
                self.along[dl] = go(piece, piece, device(x, h, c, ls(dl), y))
            self.pass_on(l)

        def pass_on(self, ll):
            for s in (2, 1, 3):
                piece = self.whole.at[y, ll]
                self.last.append(go(piece, piece, device(x, h, c, l, ys(s))))

        def relay(self):
            for dl in (1, 3, 2):
                self.along[dl].wait_recv()
                self.pass_on(ls(NL - dl))

    a0, b0 = Chunk("a", *pair0[0:8]), Chunk("b", *pair0[8:16])
    a1, b1 = Chunk("a", *pair1[0:8]), Chunk("b", *pair1[8:16])
    p0, p1 = Pair(a0, b0, True, *pair0[16:20]), Pair(a1, b1, False, *pair1[16:20])
    backward(b0.g, 0, 512)
    b0.to_core()
    backward(a0.g, 512, 512)
    a0.to_core()
    b0.first()
    a0.first()
    a1.g[...] = nn(ht[...], dcodes[:, 0:128])
    a1.to_core()
    b1.g[...] = nn(ht[...], dcodes[:, 128:256])
    b1.to_core()
    a1.first()
    b1.first()
    b0.second()
    a0.second()
    a1.second()
    b1.second()
    p0.over_z()
    p1.over_z()
    p0.spread()
    p1.spread()
    p0.relay()
    p1.relay()
    for cp in p0.last:
        cp.wait_recv()
    out0[...] = p0.whole[...]
    for cp in p1.last:
        cp.wait_recv()
    out1[...] = p1.whole[...]

    for cp in ask + to_next + to_mate + to_y + sum(reply.values(), []) + sends:
        if id(cp) not in gone:
            cp.wait_send()


def pair_scratch(width, piece, over_z):
    chunk = [
        pltpu.VMEM((1024, width), F32),
        pltpu.VMEM((4, 2, 4, 16, width), BF16),
        pltpu.VMEM((4, 2, 4, 16, width), BF16),
        pltpu.VMEM((4, 2, 4, 16, width), BF16),
        pltpu.VMEM((3, 2, 4, 16, width), BF16),
        pltpu.VMEM((2, 4, 16, width), F32),
        pltpu.VMEM((4, 2, 16, width), BF16),
        pltpu.VMEM((3, 2, 16, width), BF16),
    ]
    shared = [
        pltpu.VMEM((2, 4, *piece), F32),
        pltpu.VMEM((2, 4, *piece), over_z),
        pltpu.VMEM((8, *piece), over_z),
        pltpu.VMEM((4, 4, *piece), F32),
    ]
    return chunk + chunk + shared


def assemble(whole0, whole1, out_first, out_second):
    for yy in range(NY):
        for ll in range(NL):
            first = (1 - ll // 2) * 512 + (ll % 2) * 256
            out_first[yy * 16 : yy * 16 + 16, first : first + 256] = whole0[yy, ll]
            at = yy * 16 + (ll // 2) * 8
            out_second[at : at + 8, (ll % 2) * 128 : (ll % 2) * 128 + 128] = whole1[yy, ll]


def shards(inputs, w_first, w_second, requests, slots, counts, edge_weight, offsets):
    rows = inputs.shape[0]
    total_rows = rows * lax.axis_size("wide") * lax.axis_size("narrow")
    scale = 2.0 / (slots.shape[1] * math.sqrt(total_rows))
    vmem = pl.BlockSpec(memory_space=pltpu.VMEM)
    smem = pl.BlockSpec(memory_space=pltpu.SMEM)
    anyplace = pl.BlockSpec(memory_space=pl.ANY)
    whole0, whole1 = pl.pallas_call(
        lambda *refs: step(scale, *refs),
        out_shape=(
            jax.ShapeDtypeStruct((NY, NL, 16, 256), F32),
            jax.ShapeDtypeStruct((NY, NL, 8, 128), F32),
        ),
        in_specs=[anyplace] * 7 + [smem],
        out_specs=(vmem, vmem),
        scratch_shapes=[
            pltpu.VMEM((512, 1024), BF16),
            pltpu.VMEM((1024, 1024), BF16),
            pltpu.VMEM((1024, 256), BF16),
            pltpu.VMEM((16, 128), jnp.int32),
            pltpu.VMEM((15, 512), jnp.int32),
            pltpu.VMEM((1, 512), jnp.int32),
            pltpu.VMEM((15, 512), jnp.int32),
            pltpu.SemaphoreType.DMA((16,)),
            pltpu.VMEM((2, 8, 128, 512), BF16),
            pltpu.VMEM((512, 256), BF16),
            pltpu.VMEM((512, 1024), BF16),
            pltpu.VMEM((512, 256), F32),
            pltpu.VMEM((512, 256), BF16),
            pltpu.VMEM((512, 256), BF16),
            pltpu.VMEM((4, 512, 256), BF16),
            pltpu.VMEM((8, 8, 128), jnp.int32),
            pltpu.VMEM((8, 8, 128), jnp.int32),
            pltpu.VMEM((128, 512), F32),
            pltpu.VMEM((2, 8, 128, 256), BF16),
            pltpu.VMEM((4, 512, 256), BF16),
            pltpu.VMEM((4, 512, 128), jnp.int32),
            pltpu.VMEM((512, 128), F32),
            pltpu.VMEM((1024, 512), BF16),
            pltpu.VMEM((1024, 512), BF16),
            pltpu.VMEM((512, 128), F32),
            pltpu.VMEM((512, 256), F32),
            pltpu.VMEM((512, 512), F32),
            pltpu.VMEM((512, 512), BF16),
            pltpu.VMEM((512, 1024), BF16),
            pltpu.VMEM((512, 256), BF16),
            pltpu.VMEM((128, 128), F32),
            pltpu.VMEM((128, 128), F32),
            pltpu.SemaphoreType.DMA((128,)),
            pltpu.SemaphoreType.DMA((128,)),
        ]
        + pair_scratch(512, (16, 256), BF16)
        + pair_scratch(128, (8, 128), F32),
        compiler_params=pltpu.CompilerParams(
            collective_id=0, has_side_effects=True, vmem_limit_bytes=56 << 20
        ),
        cost_estimate=pl.CostEstimate(flops=9_000_000_000, bytes_accessed=5_000_000, transcendentals=0),
        name="embedding_step",
    )(
        inputs, w_first, w_second, requests, slots.T, counts.reshape(1, -1), edge_weight.T, offsets
    )
    return pl.pallas_call(
        assemble,
        out_shape=(jax.ShapeDtypeStruct((64, 1024), F32), jax.ShapeDtypeStruct((64, 256), F32)),
        in_specs=[vmem, vmem],
        out_specs=(vmem, vmem),
        name="assemble",
    )(whole0, whole1)


def solution(mesh):
    return jax.shard_map(
        shards,
        mesh=mesh,
        in_specs=(
            P(("wide", "narrow"), None),
            P(),
            P(),
            P(("wide", "narrow"), None),
            P(("wide", "narrow"), None),
            P(("wide", "narrow")),
            P(("wide", "narrow"), None),
            P(),
        ),
        out_specs=(P("wide", None), P("wide", None)),
        check_vma=False,
    )
```

```python
import math

import jax
import jax.numpy as jnp
from jax import lax
from jax.experimental import pallas as pl
from jax.experimental.pallas import tpu as pltpu
from jax.sharding import PartitionSpec as P

MESH = pl.DeviceIdType.MESH
F32 = jnp.float32
BF16 = jnp.bfloat16
NEGW = 8
NX, NH, NC, NL, NY = 4, 2, 2, 4, 4


def nt(a, b):
    return lax.dot_general(a, b, (((1,), (1,)), ((), ())), preferred_element_type=F32)


def nn(a, b):
    return jnp.dot(a, b, preferred_element_type=F32)


def step(
    scale, inputs_hbm, w1_hbm, w2_hbm, requests_hbm, slots_hbm, counts_hbm, edges_hbm, offsets, out0, out1,
    inputs, w1, w2, requests, slots, counts, edges, in_sem, picks, sent_part, hidden, codes, sent, mate, far, reqs, asked, keys, found, table, weights, norms,
    xt, ht, sums, acc, dist, coef, dpre, dcodes, asks_f, wishes, send_sem, recv_sem, *pairs,
):
    pair0, pair1 = pairs[:20], pairs[20:]
    w = lax.axis_index("wide")
    n = lax.axis_index("narrow")
    x, h, c = w // 4, (w // 2) % 2, w % 2
    l, y = n // 4, n % 4
    rows = inputs.shape[0]
    sem_count = [0]

    loads = []

    def load(src, dst):
        cp = pltpu.make_async_copy(src, dst, in_sem.at[len(loads)])
        cp.start()
        loads.append(cp)
        return cp

    lists = [load(slots_hbm, slots), load(counts_hbm, counts), load(edges_hbm, edges)]
    need_requests = load(requests_hbm, requests)
    need_w1 = [load(w1_hbm.at[q : q + 256], w1.at[q : q + 256]) for q in range(0, 1024, 256)]
    need_inputs = [load(inputs_hbm.at[q : q + 128], inputs.at[q : q + 128]) for q in (0, 128)]
    need_w2 = load(w2_hbm, w2)
    need_inputs += [load(inputs_hbm.at[q : q + 128], inputs.at[q : q + 128]) for q in (256, 384)]

    def device(xx, hh, cc, ll, yy):
        return (xx * 4 + hh * 2 + cc, ll * 4 + yy)

    def copy(src, dst, target):
        at = sem_count[0]
        sem_count[0] += 1
        return pltpu.make_async_remote_copy(
            src_ref=src, dst_ref=dst, send_sem=send_sem.at[at], recv_sem=recv_sem.at[at],
            device_id=target, device_id_type=MESH,
        )

    gone = []

    def left(cp):
        cp.wait_send()
        gone.append(id(cp))

    def xs(s):
        return (x + s) % NX

    def ys(s):
        return (y + s) % NY

    def ls(s):
        return (l + s) % NL

    barrier = pltpu.get_barrier_semaphore()
    plane = [(dx, dc) for dx in range(NX) for dc in range(NC) if dx or dc]
    ring = [(dl, dy) for dl in range(NL) for dy in range(NY) if dl or dy]
    peers = [device(xs(dx), h, (c + dc) % 2, l, y) for dx, dc in plane]
    peers += [device(x, h, c, ls(dl), ys(dy)) for dl, dy in ring]
    peers += [device(x, 1 - h, c, ls(dl), y) for dl in range(NL)]
    for peer in peers:
        pl.semaphore_signal(barrier, inc=1, device_id=peer, device_id_type=MESH)

    need_requests.wait()
    reqs[...] = jnp.zeros_like(reqs)
    for xx in range(NX):
        for cc in range(NC):
            for hh in range(NH):
                p = xx * 4 + hh * 2 + cc
                reqs[xx * 2 + cc, hh : hh + 1, :] = requests[p : p + 1, :]

    for cp in lists:
        cp.wait()
    live = lax.broadcasted_iota(jnp.int32, slots.shape, 0) < counts[...]
    place = ((slots[...] - x * 512) & 2047) ^ (h * 256 + c * 128)
    worth = jnp.where(live, edges[...], 0) << (((place >> 7) & 3) * 8)
    keys[...] = jnp.zeros_like(keys)
    keys[0:15, :] = (((place >> 9) << 7) | (place & 127)).astype(F32)
    keys[16:31, :] = worth.astype(F32)
    norms[...] = keys[...].T

    def weigh(at, _):
        r = pl.multiple_of(at * 16, 16)
        both = norms[pl.ds(r, 16), :].astype(jnp.int32)
        lane = lax.broadcasted_iota(jnp.int32, (16, 128), 1)
        total = [jnp.zeros((16, 128), jnp.int32) for _ in range(4)]
        for k in range(15):
            spot = jnp.broadcast_to(both[:, k : k + 1], (16, 128))
            value = jnp.broadcast_to(both[:, 16 + k : 17 + k], (16, 128))
            for part in range(4):
                total[part] = total[part] + jnp.where(spot == lane + part * 128, value, 0)
        for part in range(4):
            weights[part, pl.ds(r, 16), :] = total[part]
        return 0


    for cp in need_w1:
        cp.wait()

    def forward(half):
        for q in (2 * half, 2 * half + 1):
            need_inputs[q].wait()
            for at in range(0, 1024, 256):
                pre = nn(inputs[q * 128 : q * 128 + 128, :], w1[:, at : at + 256])
                hidden[q * 128 : q * 128 + 128, at : at + 256] = jnp.maximum(pre, 0.0).astype(BF16)
        if half == 0:
            need_w2.wait()
        some = slice(half * 256, half * 256 + 256)
        codes[some, :] = nn(hidden[some, :], w2[...])
        sent[some, :] = codes[some, :].astype(BF16)
        sent_part[some, :] = sent[some, :] * (2.0 / 256.0)

    forward(0)
    pl.semaphore_wait(barrier, len(peers))

    ask = []
    for dx, dc in plane:
        j = dx * 2 + dc
        cp = copy(reqs.at[xs(dx) * 2 + (c + dc) % 2], asked.at[j], device(xs(dx), h, (c + dc) % 2, l, y))
        cp.start()
        ask.append(cp)
    to_next = [
        copy(sent.at[at : at + 256], far.at[3, at : at + 256], device(x, h, c, ls(1), y)) for at in (0, 256)
    ]
    to_next[0].start()
    forward(1)
    to_next[1].start()
    to_mate = []
    for e in range(2):
        cols = slice(e * 128, e * 128 + 128)
        to_mate.append(copy(sent.at[:, cols], mate.at[:, cols], device(x, 1 - h, c, l, y)))
    to_mate[0].start()
    to_y = []
    for s in (1, 2, 3):
        cp = copy(sent, far.at[s - 1], device(x, h, c, l, ys(s)))
        to_y.append(cp)
        pl.when(y + s < NY)(cp.start)

    for g in range(8):
        xt[g * 128 : g * 128 + 128, :] = inputs[:, g * 128 : g * 128 + 128].T
    for cp in ask:
        cp.wait_recv()
    asked[0] = reqs[x * 2 + c]
    for j in range(8):
        norms2 = asked[j]
        asks_f[j * 8 : j * 8 + 8, :] = norms2.astype(F32)
    wishes[...] = asks_f[...].T

    lane = lax.broadcasted_iota(jnp.int32, (128, rows), 1).astype(F32)
    reply = {}

    def deliver(block, b, e):
        cols = slice(0, 256) if e is None else slice(e * 128, e * 128 + 128)
        got = nn(picks[b].reshape(8 * 128, rows), block[:, cols]).astype(BF16)
        found[b, :, :, cols] = got.reshape(8, 128, got.shape[1])
        for j in turns:
            dx, dc = j // 2, j % 2
            spot = slice(b * 256 + dc * 128, b * 256 + dc * 128 + 128)
            if j == 0:
                table[0, spot, cols] = found[b, 0, :, cols]
            else:
                cp = copy(
                    found.at[b, j, :, cols], table.at[dx, spot, cols],
                    device(xs(NX - dx), h, (c + dc) % 2, l, y),
                )
                cp.start()
                reply.setdefault((b, dx), []).append(cp)

    turns = (4, 5, 2, 6, 3, 7, 1, 0)

    def choose(b):
        for j in turns:
            which = jnp.where((h + b) % 2 == 0, wishes[:, j * 8 : j * 8 + 1], wishes[:, j * 8 + 1 : j * 8 + 2])
            picks[b, j] = jnp.where(jnp.broadcast_to(which, (128, rows)) == lane, 1.0, 0.0).astype(BF16)

    choose(0)
    deliver(sent, 0, None)
    for cp in to_next:
        left(cp)
    to_mate[1].start()
    for cp in to_next:
        cp.wait_recv()
    for s in (1, 2, 3):
        cp = pltpu.make_async_remote_copy(
            src_ref=far.at[3], dst_ref=far.at[s - 1], send_sem=send_sem.at[11 + s - 1],
            recv_sem=recv_sem.at[11 + s - 1], device_id=device(x, h, c, l, ys(s)), device_id_type=MESH,
        )
        pl.when(y + s >= NY)(cp.start)
    lax.fori_loop(0, rows // 16, weigh, 0)
    choose(1)
    for g in range(8):
        ht[g * 128 : g * 128 + 128, :] = hidden[:, g * 128 : g * 128 + 128].T

    inv = 1.0 / 256.0
    own = sent[...].astype(F32)
    norm = jnp.sum(own * own, axis=1, keepdims=True)
    norms[...] = jnp.broadcast_to(norm * inv + 1.0, norms.shape)
    sums[...] = jnp.zeros_like(sums)
    acc[...] = jnp.zeros_like(acc)
    ones = jnp.ones((8, 256), BF16)

    def squares(block):
        z = block.astype(F32)
        z = z * z
        hi = z.astype(BF16)
        lo = (z - hi.astype(F32)).astype(BF16)
        return (nt(ones, hi) + nt(ones, lo))[0:1, :] * inv

    def pull(block, dx, b, offset):
        wide = block.shape[0]
        dist[:, 0:wide] = nt(sent_part[...], block[...])
        size = squares(block[...])

        def tile(at, _):
            r = pl.multiple_of(at * 64, 64)
            mine = norms[pl.ds(r, 64), :]
            total = sums[pl.ds(r, 64), :]
            for q in range(wide // 128):
                cols = slice(q * 128, q * 128 + 128)
                d = jnp.maximum((mine + size[:, cols]) - dist[pl.ds(r, 64), cols], 1.0)
                if dx is not None:
                    count = (weights[dx, pl.ds(r, 64), :] >> (8 * (b * 2 + q))) & 255
                    k = count.astype(F32) * (1.0 / d)
                else:
                    i = lax.broadcasted_iota(jnp.int32, (64, 128), 0)
                    j = lax.broadcasted_iota(jnp.int32, (64, 128), 1)
                    band = ((j - i) + (q * 128 - r - offset)) & (rows - 1)
                    k = jnp.where(band < NEGW, -1.0 / (d * (1.1 * (d - 1.0) + 0.1)), 0.0)
                k = k.astype(BF16)
                coef[pl.ds(r, 64), cols] = k
                total = total + k.astype(F32)
            sums[pl.ds(r, 64), :] = total
            return 0

        lax.fori_loop(0, rows // 64, tile, 0)
        acc[...] += nn(coef[:, 0:wide], block[...])

    def attract(b):
        for dx in (0, 1, 3, 2):
            for cp in reply[b, dx]:
                cp.wait_recv()
            pull(table.at[dx, b * 256 : b * 256 + 256], dx, b, None)

    def serve_mate(e):
        to_mate[e].wait_recv()
        deliver(mate, 1, e)

    attract(0)
    serve_mate(0)
    pull(far.at[3], None, None, offsets[3])
    serve_mate(1)
    for s in (1, 3, 2):
        to_y[s - 1].wait_recv()
        pull(far.at[s - 1], None, None, offsets[s - 1])
    attract(1)

    total = jnp.sum(sums[...], axis=1, keepdims=True)
    dcodes[...] = (scale * (total * codes[...] - acc[...])).astype(BF16)

    core = device(x, h, 1 - c, l, y)

    def backward(g, first, width):
        for at in range(first, first + width, 128):
            back = nt(dcodes[...], w2[at : at + 128, :])
            dpre[:, at : at + 128] = jnp.where(hidden[:, at : at + 128] > 0, back, 0.0).astype(BF16)
        g[...] = nn(xt[...], dpre[:, first : first + width])

    def part_rows(xx, hh, cc, yy):
        return pl.ds(pl.multiple_of(xx * 256 + hh * 128 + cc * 64 + yy * 16, 16), 16)

    each = [(xx, hh, yy) for xx in range(NX) for hh in range(NH) for yy in range(NY)]
    sends = []

    def go(src, dst, target):
        cp = copy(src, dst, target)
        cp.start()
        sends.append(cp)
        return cp

    def spot(kind, xx, hh, yy):
        return (xx, hh, yy) if kind == "a" else (yy, hh, xx)

    class Chunk:
        def __init__(self, kind, g, c_out, c_in, p_out, p_in, f, q_out, q_in):
            self.kind, self.g, self.c_out, self.c_in, self.p_out, self.p_in = kind, g, c_out, c_in, p_out, p_in
            self.f, self.q_out, self.q_in = f, q_out, q_in

        def near(self, s):
            return (xs(s), device(xs(s), h, c, l, y)) if self.kind == "a" else (ys(s), device(x, h, c, l, ys(s)))

        def beyond(self, s):
            return (ys(s), device(x, h, c, l, ys(s))) if self.kind == "a" else (xs(s), device(xs(s), h, c, l, y))

        def to_core(self):
            for xx, hh, yy in each:
                self.c_out[spot(self.kind, xx, hh, yy)] = self.g[part_rows(xx, hh, 1 - c, yy), :].astype(BF16)
            self.core = go(self.c_out, self.c_in, core)

        def first(self):
            self.core.wait_recv()
            self.one = []
            for s in (2, 1, 3):
                at, target = self.near(s)
                for hh in range(NH):
                    for k in range(4):
                        rows_at = part_rows(at, hh, c, k) if self.kind == "a" else part_rows(k, hh, c, at)
                        both = self.g[rows_at, :] + self.c_in[at, hh, k].astype(F32)
                        self.p_out[at, hh, k] = both.astype(BF16)
                self.one.append(go(self.p_out.at[at], self.p_in.at[s - 1], target))
            mine = x if self.kind == "a" else y
            for far_at in range(4):
                for hh in range(NH):
                    rows_at = part_rows(x, hh, c, far_at) if self.kind == "a" else part_rows(far_at, hh, c, y)
                    self.f[hh, far_at] = self.g[rows_at, :] + self.c_in[mine, hh, far_at].astype(F32)

        def second(self):
            for cp in self.one:
                cp.wait_recv()
            for hh in range(NH):
                for far_at in range(4):
                    got = [self.p_in[s, hh, far_at].astype(F32) for s in range(3)]
                    self.f[hh, far_at] += got[0] + got[1] + got[2]
                    self.q_out[far_at, hh] = self.f[hh, far_at].astype(BF16)
            self.two = []
            for s in (2, 1, 3):
                at, target = self.beyond(s)
                self.two.append(go(self.q_out.at[at], self.q_in.at[s - 1], target))

        def result(self, hh):
            mine = y if self.kind == "a" else x
            got = [self.q_in[s, hh].astype(F32) for s in range(3)]
            return self.f[hh, mine] + got[0] + got[1] + got[2]

    class Pair:
        def __init__(self, a, b, by_columns, zs_own, zs_out, zs_in, whole):
            self.a, self.b, self.by_columns, self.zs_own = a, b, by_columns, zs_own
            self.zs_out, self.zs_in, self.whole = zs_out, zs_in, whole

        def over_z(self):
            for cp in self.a.two + self.b.two:
                cp.wait_recv()
            for hh in range(NH):
                for half, chunk in enumerate((self.a, self.b)):
                    total = chunk.result(hh)
                    if self.by_columns:
                        pieces = ((2 * half, total[:, 0:256]), (2 * half + 1, total[:, 256:512]))
                    else:
                        pieces = ((half, total[0:8, :]), (2 + half, total[8:16, :]))
                    for ll, piece in pieces:
                        self.zs_own[hh, ll] = piece
                        self.zs_out[hh, ll] = piece.astype(self.zs_out.dtype)
            self.zs = []
            for dh, dl in ((1, 0), (1, 2), (1, 1), (1, 3), (0, 2), (0, 1), (0, 3)):
                hh = (h + dh) % 2
                self.zs.append(
                    go(self.zs_out.at[hh, ls(dl)], self.zs_in.at[dh * 4 + dl], device(x, hh, c, ls(dl), y))
                )

        def spread(self):
            total = self.zs_own[h, l]
            for cp in self.zs:
                cp.wait_recv()
            for k in range(1, 8):
                total = total + self.zs_in[k].astype(F32)
            self.whole[y, l] = total
            self.along = {}
            self.last = []
            for dl in (2, 1, 3):
                piece = self.whole.at[y, l]
                self.along[dl] = go(piece, piece, device(x, h, c, ls(dl), y))
            self.pass_on(l)

        def pass_on(self, ll):
            for s in (2, 1, 3):
                piece = self.whole.at[y, ll]
                self.last.append(go(piece, piece, device(x, h, c, l, ys(s))))

        def relay(self):
            for dl in (1, 3, 2):
                self.along[dl].wait_recv()
                self.pass_on(ls(NL - dl))

    a0, b0 = Chunk("a", *pair0[0:8]), Chunk("b", *pair0[8:16])
    a1, b1 = Chunk("a", *pair1[0:8]), Chunk("b", *pair1[8:16])
    p0, p1 = Pair(a0, b0, True, *pair0[16:20]), Pair(a1, b1, False, *pair1[16:20])
    backward(b0.g, 0, 512)
    b0.to_core()
    backward(a0.g, 512, 512)
    a0.to_core()
    b0.first()
    a0.first()
    a1.g[...] = nn(ht[...], dcodes[:, 0:128])
    a1.to_core()
    b1.g[...] = nn(ht[...], dcodes[:, 128:256])
    b1.to_core()
    a1.first()
    b1.first()
    b0.second()
    a0.second()
    a1.second()
    b1.second()
    p0.over_z()
    p1.over_z()
    p0.spread()
    p1.spread()
    p0.relay()
    p1.relay()
    for cp in p0.last:
        cp.wait_recv()
    out0[...] = p0.whole[...]
    for cp in p1.last:
        cp.wait_recv()
    out1[...] = p1.whole[...]

    for cp in ask + to_next + to_mate + to_y + sum(reply.values(), []) + sends:
        if id(cp) not in gone:
            cp.wait_send()


def pair_scratch(width, piece, over_z):
    chunk = [
        pltpu.VMEM((1024, width), F32),
        pltpu.VMEM((4, 2, 4, 16, width), BF16),
        pltpu.VMEM((4, 2, 4, 16, width), BF16),
        pltpu.VMEM((4, 2, 4, 16, width), BF16),
        pltpu.VMEM((3, 2, 4, 16, width), BF16),
        pltpu.VMEM((2, 4, 16, width), F32),
        pltpu.VMEM((4, 2, 16, width), BF16),
        pltpu.VMEM((3, 2, 16, width), BF16),
    ]
    shared = [
        pltpu.VMEM((2, 4, *piece), F32),
        pltpu.VMEM((2, 4, *piece), over_z),
        pltpu.VMEM((8, *piece), over_z),
        pltpu.VMEM((4, 4, *piece), F32),
    ]
    return chunk + chunk + shared


def assemble(whole0, whole1, out_first, out_second):
    for yy in range(NY):
        for ll in range(NL):
            first = (1 - ll // 2) * 512 + (ll % 2) * 256
            out_first[yy * 16 : yy * 16 + 16, first : first + 256] = whole0[yy, ll]
            at = yy * 16 + (ll // 2) * 8
            out_second[at : at + 8, (ll % 2) * 128 : (ll % 2) * 128 + 128] = whole1[yy, ll]


def shards(inputs, w_first, w_second, requests, slots, counts, edge_weight, offsets):
    rows = inputs.shape[0]
    total_rows = rows * lax.axis_size("wide") * lax.axis_size("narrow")
    scale = 2.0 / (slots.shape[1] * math.sqrt(total_rows))
    vmem = pl.BlockSpec(memory_space=pltpu.VMEM)
    smem = pl.BlockSpec(memory_space=pltpu.SMEM)
    anyplace = pl.BlockSpec(memory_space=pl.ANY)
    whole0, whole1 = pl.pallas_call(
        lambda *refs: step(scale, *refs),
        out_shape=(
            jax.ShapeDtypeStruct((NY, NL, 16, 256), F32),
            jax.ShapeDtypeStruct((NY, NL, 8, 128), F32),
        ),
        in_specs=[anyplace] * 7 + [smem],
        out_specs=(vmem, vmem),
        scratch_shapes=[
            pltpu.VMEM((512, 1024), BF16),
            pltpu.VMEM((1024, 1024), BF16),
            pltpu.VMEM((1024, 256), BF16),
            pltpu.VMEM((16, 128), jnp.int32),
            pltpu.VMEM((15, 512), jnp.int32),
            pltpu.VMEM((1, 512), jnp.int32),
            pltpu.VMEM((15, 512), jnp.int32),
            pltpu.SemaphoreType.DMA((16,)),
            pltpu.VMEM((2, 8, 128, 512), BF16),
            pltpu.VMEM((512, 256), BF16),
            pltpu.VMEM((512, 1024), BF16),
            pltpu.VMEM((512, 256), F32),
            pltpu.VMEM((512, 256), BF16),
            pltpu.VMEM((512, 256), BF16),
            pltpu.VMEM((4, 512, 256), BF16),
            pltpu.VMEM((8, 8, 128), jnp.int32),
            pltpu.VMEM((8, 8, 128), jnp.int32),
            pltpu.VMEM((128, 512), F32),
            pltpu.VMEM((2, 8, 128, 256), BF16),
            pltpu.VMEM((4, 512, 256), BF16),
            pltpu.VMEM((4, 512, 128), jnp.int32),
            pltpu.VMEM((512, 128), F32),
            pltpu.VMEM((1024, 512), BF16),
            pltpu.VMEM((1024, 512), BF16),
            pltpu.VMEM((512, 128), F32),
            pltpu.VMEM((512, 256), F32),
            pltpu.VMEM((512, 512), F32),
            pltpu.VMEM((512, 512), BF16),
            pltpu.VMEM((512, 1024), BF16),
            pltpu.VMEM((512, 256), BF16),
            pltpu.VMEM((128, 128), F32),
            pltpu.VMEM((128, 128), F32),
            pltpu.SemaphoreType.DMA((128,)),
            pltpu.SemaphoreType.DMA((128,)),
        ]
        + pair_scratch(512, (16, 256), BF16)
        + pair_scratch(128, (8, 128), F32),
        compiler_params=pltpu.CompilerParams(
            collective_id=0, has_side_effects=True, vmem_limit_bytes=56 << 20
        ),
        cost_estimate=pl.CostEstimate(flops=9_000_000_000, bytes_accessed=5_000_000, transcendentals=0),
        name="embedding_step",
    )(
        inputs, w_first, w_second, requests, slots.T, counts.reshape(1, -1), edge_weight.T, offsets
    )
    return pl.pallas_call(
        assemble,
        out_shape=(jax.ShapeDtypeStruct((64, 1024), F32), jax.ShapeDtypeStruct((64, 256), F32)),
        in_specs=[vmem, vmem],
        out_specs=(vmem, vmem),
        name="assemble",
    )(whole0, whole1)


def solution(mesh):
    return jax.shard_map(
        shards,
        mesh=mesh,
        in_specs=(
            P(("wide", "narrow"), None),
            P(),
            P(),
            P(("wide", "narrow"), None),
            P(("wide", "narrow"), None),
            P(("wide", "narrow")),
            P(("wide", "narrow"), None),
            P(),
        ),
        out_specs=(P("wide", None), P("wide", None)),
        check_vma=False,
    )
```
